512 devices in a mesh: ens: 8 (over z_hi, x), node: 64 (over y, z_lo, core).
Axes of the slice: x: 4, y: 4, z: 16 (z_hi: 2, z_lo: 8; z = z_hi * 8 + z_lo), core: 2. Of those that a mesh axis runs over, the one named last changes fastest.
Arguments:
- latent: bfloat16 [8, 8192, 1024], P('ens', 'node'), may hold values from -48 to 48, as said below
- gain: float32 [1024], replicated, may hold values from 0.1 to 1.9
- w_query: bfloat16 [1024, 1024], P('node'), may hold values from -0.1875 to 0.1875
- w_key: bfloat16 [1024, 1024], P('node'), may hold values from -0.1875 to 0.1875
- w_value: bfloat16 [1024, 1024], P('node'), may hold values from -0.1875 to 0.1875
- w_read: bfloat16 [1024, 128], replicated, may hold values from -0.1875 to 0.1875
- target: float32 [8192, 128], P('node'), may hold values from -6 to 6
- neighbours: int32 [8192, 8], P('node'), may hold values from 0 to 8191, as said below
- slot_mask: int32 [8192, 8], P('node'), may hold values from 0 to 1, as said below
Outputs:
- crps: float32 [8192, 128], P('node', 'ens')
- grad_latent: float32 [8, 8192, 1024], P('ens', 'node')
The draws below stay inside these ranges and needn't reach their ends.
Inputs may be any that keep to these rules, and one draw needn't show every extreme that they name: `latent`: positive and negative activations; the scale varies from node to node and from feature to feature. `neighbours`: slot 0 of node i holds i. Every entry lies within 64 places of its own node in the cyclic node order; some nodes reach exactly 64 on either side. Unused slots hold the node itself. `slot_mask`: slots 0 and 1 are used in every row; the used slots of a row come first.
All inputs are finite; a program needn't handle non-finite values.
Results may differ from the reference program's by a relative error of at most 0.03.
Values may be sent and summed in bfloat16 or wider, within the bound.
A program may use at most 64 MiB of HBM per device.

```python
import jax
import jax.numpy as jnp
from jax import lax

D = 1024
HEAD_DIM = 64
V = 128
SLOTS = 8
HALO = 64
NODES_DEV = 128
NODES = 8192
MEMBERS = 8


def neighbour_table(key):
    key_reach, key_sign, key_count = jax.random.split(key, 3)
    base = jnp.arange(NODES, dtype=jnp.int32)
    reach = jax.random.randint(key_reach, (NODES, SLOTS), 1, HALO + 1)
    signs = jax.random.randint(key_sign, (NODES, SLOTS), 0, 2) * 2 - 1
    offset = reach * signs
    place = base % NODES_DEV
    forced = jnp.where(place == 0, -HALO, jnp.where(place == NODES_DEV - 1, HALO, offset[:, 1]))
    offset = offset.at[:, 1].set(forced)
    counts = jax.random.randint(key_count, (NODES,), 2, SLOTS + 1)
    slot_index = jnp.arange(SLOTS, dtype=jnp.int32)
    valid = slot_index[None, :] < counts[:, None]
    ids = (base[:, None] + offset + NODES) % NODES
    ids = jnp.where(valid, ids, base[:, None])
    ids = ids.at[:, 0].set(base)
    return (ids.astype(jnp.int32), valid.astype(jnp.int32))


def draw_neighbours(key, part):
    table = neighbour_table(key)
    return table[0]


def draw_slot_mask(key, part):
    table = neighbour_table(key)
    return table[1]


def draw_latent(key, part):
    key = jax.random.fold_in(key, 7)
    key_base, key_rows, key_cols = jax.random.split(key, 3)
    row_scale = jnp.exp(jax.random.uniform(key_rows, (MEMBERS, NODES, 1), minval=-1.2, maxval=1.2))
    col_scale = jnp.exp(jax.random.uniform(key_cols, (1, 1, D), minval=-1.2, maxval=1.2))
    base = jnp.clip(jax.random.normal(key_base, (MEMBERS, NODES, D)), -4.0, 4.0)
    return (base * row_scale * col_scale).astype(jnp.bfloat16)


def steps_of(key, shape, pieces, smallest, largest):
    level = 1.0
    for dim, shards_of in pieces:
        steps = jax.random.uniform(jax.random.fold_in(jax.random.fold_in(key, 6), dim), (shards_of,), jnp.float32, smallest / len(pieces), largest / len(pieces))
        level = level * jnp.repeat(jnp.exp(steps), shape[dim] // shards_of).reshape((-1,) + (1,) * (len(shape) - 1 - dim))
    return level


def scatter_about(key, shape, scale, bound, pieces=(), held_as=jnp.bfloat16):
    drawn = scale * jax.random.normal(key, shape, jnp.float32)
    if pieces:
        drawn = drawn * steps_of(key, shape, pieces, -0.22, 0.18)
    return jnp.clip(drawn, -bound, bound).astype(held_as)


def setup_inputs(seed: int = 0) -> dict:
    key_of = jax.random.split(jax.random.key(seed), 10)
    return {
        "latent": draw_latent(jax.random.fold_in(key_of[9], 71), 0),
        "gain": jnp.clip(1.0 + 0.18 * jax.random.normal(key_of[1], (D,), jnp.float32), 0.1, 1.9),
        "w_query": scatter_about(key_of[2], (D, D), D ** -0.5, 0.1875, ((0, 64),)),
        "w_key": scatter_about(key_of[3], (D, D), D ** -0.5, 0.1875, ((0, 64),)),
        "w_value": scatter_about(key_of[4], (D, D), D ** -0.5, 0.1875, ((0, 64),)),
        "w_read": scatter_about(key_of[5], (D, V), D ** -0.5, 0.1875),
        "target": scatter_about(key_of[6], (NODES, V), 1.0, 6.0, ((0, 64),), jnp.float32),
        "neighbours": draw_neighbours(jax.random.fold_in(key_of[9], 71), 0),
        "slot_mask": draw_slot_mask(jax.random.fold_in(key_of[9], 71), 0),
    }


EPSILON = 1e-06
SOFTNESS = 0.1

def smooth_abs(gap):
    return jnp.sqrt(gap * gap + SOFTNESS * SOFTNESS)

def smooth_sign(gap):
    return gap / jnp.sqrt(gap * gap + SOFTNESS * SOFTNESS)

def rms_parts(member_latent, gain):
    widened = member_latent.astype(jnp.float32)
    inverse = lax.rsqrt(lax.optimization_barrier(jnp.mean(widened * widened, axis=-1, keepdims=True)) + EPSILON)
    normed = (widened * inverse * gain).astype(jnp.bfloat16)
    return (widened, inverse, normed)

def attend_block(own_query, keys_near, values_near, valid):
    count = own_query.shape[0]
    width = own_query.shape[1]
    heads = width // HEAD_DIM
    query_h = own_query.astype(jnp.float32).reshape(count, heads, HEAD_DIM)
    key_h = keys_near.astype(jnp.float32).reshape(count, SLOTS, heads, HEAD_DIM)
    value_h = values_near.astype(jnp.float32).reshape(count, SLOTS, heads, HEAD_DIM)
    scores = jnp.einsum('bhd,bkhd->bkh', query_h, key_h) * HEAD_DIM ** (-0.5)
    weights = jnp.where(valid[:, :, None], jnp.exp(scores), 0.0)
    probs = weights / lax.optimization_barrier(jnp.sum(weights, axis=1, keepdims=True))
    rounded = probs.astype(jnp.bfloat16)
    mixed = jnp.einsum('bkh,bkhd->bhd', rounded.astype(jnp.float32), value_h).reshape(count, width)
    return (probs, rounded, mixed, query_h, key_h, value_h)

def forward_member(member_latent, gain, w_query, w_key, w_value, w_read, neighbours, valid):
    widened, inverse, normed = rms_parts(member_latent, gain)
    queries = jnp.dot(normed, w_query, preferred_element_type=jnp.float32).astype(jnp.bfloat16)
    keys = jnp.dot(normed, w_key, preferred_element_type=jnp.float32).astype(jnp.bfloat16)
    values = jnp.dot(normed, w_value, preferred_element_type=jnp.float32).astype(jnp.bfloat16)
    width = member_latent.shape[1]
    blocks = member_latent.shape[0] // NODES_DEV

    def one_block(index):
        first = (index * NODES_DEV).astype(jnp.int32)
        ids = lax.dynamic_slice_in_dim(neighbours, first, NODES_DEV, 0)
        mask_rows = lax.dynamic_slice_in_dim(valid, first, NODES_DEV, 0)
        own = lax.dynamic_slice_in_dim(queries, first, NODES_DEV, 0)
        outcome = attend_block(own, keys[ids], values[ids], mask_rows)
        return outcome[2]
    mixed = lax.map(one_block, jnp.arange(blocks, dtype=jnp.int32)).reshape(-1, width)
    updated = (widened + mixed).astype(jnp.bfloat16)
    field = jnp.dot(updated, w_read, preferred_element_type=jnp.float32)
    return (field, queries, keys, values)

def backward_member(member_latent, pull, queries, keys, values, gain, w_query, w_key, w_value, w_read, neighbours, valid):
    widened, inverse, normed = rms_parts(member_latent, gain)
    nodes = member_latent.shape[0]
    width = member_latent.shape[1]
    heads = width // HEAD_DIM
    blocks = nodes // NODES_DEV
    contract = (((1,), (1,)), ((), ()))
    down = lax.dot_general(pull.astype(jnp.bfloat16), w_read, contract, preferred_element_type=jnp.float32)
    down_b = down.astype(jnp.bfloat16)

    def one_block(carry, index):
        key_grad, value_grad = carry
        first = (index * NODES_DEV).astype(jnp.int32)
        ids = lax.dynamic_slice_in_dim(neighbours, first, NODES_DEV, 0)
        mask_rows = lax.dynamic_slice_in_dim(valid, first, NODES_DEV, 0)
        own = lax.dynamic_slice_in_dim(queries, first, NODES_DEV, 0)
        own_down = lax.dynamic_slice_in_dim(down_b, first, NODES_DEV, 0)
        probs, rounded, mixed, query_h, key_h, value_h = attend_block(own, keys[ids], values[ids], mask_rows)
        grad_h = own_down.astype(jnp.float32).reshape(NODES_DEV, heads, HEAD_DIM)
        dprob = jnp.einsum('bhd,bkhd->bkh', grad_h, value_h)
        dscore = probs * (dprob - lax.optimization_barrier(jnp.sum(probs * dprob, axis=1, keepdims=True)))
        dscaled = (dscore * HEAD_DIM ** (-0.5)).astype(jnp.bfloat16).astype(jnp.float32)
        dquery = jnp.einsum('bkh,bkhd->bhd', dscaled, key_h).reshape(NODES_DEV, width).astype(jnp.bfloat16)
        dkey = jnp.einsum('bkh,bhd->bkhd', dscaled, query_h).reshape(NODES_DEV * SLOTS, width)
        dvalue = jnp.einsum('bkh,bhd->bkhd', rounded.astype(jnp.float32), grad_h).reshape(NODES_DEV * SLOTS, width)
        flat = ids.reshape(-1)
        return ((key_grad.at[flat].add(dkey), value_grad.at[flat].add(dvalue)), dquery)
    zeros = jnp.zeros((nodes, width), jnp.float32)
    sums, dquery = lax.scan(one_block, (zeros, zeros), jnp.arange(blocks, dtype=jnp.int32))
    dquery = dquery.reshape(nodes, width)
    key_grad = sums[0].astype(jnp.bfloat16)
    value_grad = sums[1].astype(jnp.bfloat16)
    back = lax.dot_general(dquery, w_query, contract, preferred_element_type=jnp.float32)
    back = back + lax.dot_general(key_grad, w_key, contract, preferred_element_type=jnp.float32)
    back = back + lax.dot_general(value_grad, w_value, contract, preferred_element_type=jnp.float32)
    scaled = back * gain
    norm_back = inverse * scaled - widened * inverse * inverse * inverse * lax.optimization_barrier(jnp.mean(scaled * widened, axis=-1, keepdims=True))
    return down + norm_back

def reference(latent, gain, w_query, w_key, w_value, w_read, target, neighbours, slot_mask):
    valid = slot_mask > 0
    members = latent.shape[0]

    def forward_one(member_latent):
        return forward_member(member_latent, gain, w_query, w_key, w_value, w_read, neighbours, valid)
    fields, queries, keys, values = lax.map(forward_one, latent)

    def pair_sums(field):
        gaps = field[None] - fields
        return (lax.optimization_barrier(jnp.sum(smooth_abs(gaps), axis=0)), lax.optimization_barrier(jnp.sum(smooth_sign(gaps), axis=0)))
    spreads, pulls = lax.map(pair_sums, fields)
    crps = lax.optimization_barrier(jnp.mean(smooth_abs(fields - target[None]), axis=0)) - lax.optimization_barrier(jnp.sum(spreads, axis=0)) / (2.0 * members * (members - 1))
    pull = smooth_sign(fields - target[None]) - pulls / (members - 1)

    def backward_one(packed):
        return backward_member(packed[0], packed[1], packed[2], packed[3], packed[4], gain, w_query, w_key, w_value, w_read, neighbours, valid)
    grad_latent = lax.map(backward_one, (latent, pull, queries, keys, values))
    return (crps, grad_latent)
```

```python
import jax
import jax.numpy as jnp
from jax import lax
from jax.experimental import pallas as pl
from jax.experimental.pallas import tpu as pltpu
from jax.sharding import PartitionSpec as P

HEAD_DIM = 64
SLOTS = 8
HALO = 64
EPSILON = 1e-06
SOFTNESS = 0.1

D = 1024
V = 128
ROWS = 128
PAIR = 2 * ROWS
NEAR = PAIR + 2 * HALO
HALF = D // 2
WINDOW = ROWS + 2 * HALO
GROUPS = HALF // 128
MEMBERS = 8
X, Y, Z, Z_LO = 4, 4, 16, 8
CHIPS = Y * Z_LO
MESH = pl.DeviceIdType.MESH
COPIES = 160

F32 = jnp.float32
BF16 = jnp.bfloat16
NT = (((1,), (1,)), ((), ()))
TN = (((0,), (0,)), ((), ()))


def dot(a, b):
    return jnp.dot(a, b, preferred_element_type=F32)


def dot_nt(a, b):
    return lax.dot_general(a, b, NT, preferred_element_type=F32)


def dot_tn(a, b):
    return lax.dot_general(a, b, TN, preferred_element_type=F32)


class Place:
    def __init__(self):
        self.member = lax.axis_index("ens")
        self.node = lax.axis_index("node")
        self.x = self.member % X
        self.y = self.node // (2 * Z_LO)
        self.z = (self.member // X) * Z_LO + (self.node // 2) % Z_LO
        self.core = self.node % 2

    def at(self, dx=0, dy=0, dz=0, dc=0):
        x, y, z = (self.x + dx + X) % X, (self.y + dy + Y) % Y, (self.z + dz + Z) % Z
        core = (self.core + dc) % 2
        return {"ens": (z // Z_LO) * X + x, "node": (y * Z_LO + z % Z_LO) * 2 + core}

    def chip(self, step, core):
        return {"ens": self.member, "node": ((self.node // 2 + step + CHIPS) % CHIPS) * 2 + core}


class Net:
    def __init__(self, send_sem, recv_sem):
        self.send_sem, self.recv_sem = send_sem, recv_sem
        self.count = 0
        self.sent = []

    def send(self, src, dst, to):
        copy = pltpu.make_async_remote_copy(
            src_ref=src,
            dst_ref=dst,
            send_sem=self.send_sem.at[self.count],
            recv_sem=self.recv_sem.at[self.count],
            device_id=to,
            device_id_type=MESH,
        )
        self.count += 1
        copy.start()
        self.sent.append(copy)
        return copy

    def drain(self):
        for copy in self.sent:
            copy.wait_send()


def gather_weights(here, net, w_refs, W, local_sem):
    y, z, c = here.y, here.z % Z_LO, here.core
    mine, other = pl.multiple_of(c * HALF, HALF), pl.multiple_of((1 - c) * HALF, HALF)
    own_rows = pl.ds(pl.multiple_of(c * 16, 16), 16)
    local, swap = [], []
    for i, w in enumerate(w_refs):
        spot = W.at[i, y, z, own_rows]
        swap.append(net.send(w.at[:, pl.ds(other, HALF)], spot, here.at(dc=1)))
        local.append(pltpu.make_async_copy(w.at[:, pl.ds(mine, HALF)], spot, local_sem.at[i]))
        local[-1].start()
    for copy in local:
        copy.wait()
    for copy in swap:
        copy.wait_recv()

    first, second = pl.ds(0, 16), pl.ds(16, 16)
    kept = pl.ds(here.x % 2, 2)
    given = (here.x % 2) * 2
    across = []

    def pass_on(rows, ys, zs):
        piece = W.at[given, ys, zs, rows]
        across.append(net.send(piece, piece, here.at(dx=1 if rows is first else -1)))

    def forward(ys, zs, rows, **step):
        piece = W.at[kept, ys, zs, rows]
        return net.send(piece, piece, here.at(**step))

    every = slice(None)
    below, above, far = (y + 3) % Y, (y + 1) % Y, (y + 2) % Y
    along_y = [forward(y, z, first, dy=d) for d in (1, -1, 2)]
    second_up, second_down = forward(y, z, second, dz=1), forward(y, z, second, dz=-1)
    pending = [(z, forward(y, z, second, dy=1), forward(y, z, second, dy=-1))]
    for copy in along_y:
        copy.wait_recv()
    first_up, first_down = forward(every, z, first, dz=1), forward(every, z, first, dz=-1)
    for ys in (below, above, far):
        pass_on(first, ys, z)
    relayed = []

    def spread(zs, from_below, from_above):
        from_below.wait_recv()
        from_above.wait_recv()
        if len(relayed) % 2 == 0:
            relayed.append((zs, forward(below, zs, second, dy=1)))
        else:
            relayed.append((zs, forward(above, zs, second, dy=-1)))
        for ys in (below, above) if zs is z else (below, above, y):
            pass_on(second, ys, zs)

    last = Z_LO // 2
    for step in range(1, last + 1):
        before, after = (z + Z_LO - step) % Z_LO, (z + step) % Z_LO
        arrived = []
        if step < last:
            second_up.wait_recv()
            if step < last - 1:
                second_up = forward(y, before, second, dz=1)
            arrived.append((before, forward(y, before, second, dy=1), forward(y, before, second, dy=-1)))
        second_down.wait_recv()
        if step < last:
            second_down = forward(y, after, second, dz=-1)
        arrived.append((after, forward(y, after, second, dy=1), forward(y, after, second, dy=-1)))
        first_up.wait_recv()
        first_down.wait_recv()
        if step < last - 1:
            first_up, first_down = forward(every, before, first, dz=1), forward(every, after, first, dz=-1)
        elif step == last - 1:
            first_up = forward(pl.ds(0, 2), before, first, dz=1)
            first_down = forward(pl.ds(2, 2), after, first, dz=-1)
        if step < last:
            pass_on(first, every, before)
        pass_on(first, every, after)
        for item in pending:
            spread(*item)
        pending = arrived
    for item in pending:
        spread(*item)
    for zs, copy in relayed:
        copy.wait_recv()
        pass_on(second, far, zs)
    for copy in across:
        copy.wait_recv()


def body(
    latent, gain, w_query, w_key, w_value, w_read, target, neighbours, slot_mask,
    crps_out, grad_out,
    W, near, normed, inverse, counts, queries, keys, values, probs, mixed,
    part, part_in, field, pull, down, dquery, dkey, dvalue, halo_out, halo_in, back, back_in,
    send_sem, recv_sem, local_sem,
):
    here = Place()
    net = Net(send_sem, recv_sem)
    core = here.core
    peers = [
        here.at(dc=1),
        here.at(dy=1), here.at(dy=-1), here.at(dy=2),
        here.at(dz=1), here.at(dz=-1), here.at(dz=8),
        here.at(dx=1), here.at(dx=-1), here.at(dx=2),
        here.chip(1, core), here.chip(-1, core), here.chip(2 * core - 1, 1 - core),
    ]
    barrier = pltpu.get_barrier_semaphore()
    for peer in peers:
        pl.semaphore_signal(barrier, inc=1, device_id=peer, device_id_type=MESH)
    pl.semaphore_wait(barrier, len(peers))

    own = pl.ds(pl.multiple_of(HALO + core * ROWS, 64), ROWS)
    edge = pl.ds(pl.multiple_of(core * HALO, 64), HALO)
    edge_there = pl.ds(pl.multiple_of((1 - core) * (HALO + PAIR), 64), HALO)
    edge_here = pl.ds(pl.multiple_of(core * (HALO + PAIR), 64), HALO)
    own_copy = pltpu.make_async_copy(latent, near.at[own], local_sem.at[3])
    own_copy.start()
    pair_copy = net.send(latent, near.at[own], here.at(dc=1))
    edge_copy = net.send(latent.at[edge], near.at[edge_there], here.chip(2 * core - 1, 1 - core))

    first = here.node * ROWS - HALO
    total = 2 * CHIPS * ROWS
    spot = neighbours[...] - first
    spot = jnp.where(spot < 0, spot + total, spot)
    spot = jnp.where(spot >= total, spot - total, spot)
    used = (slot_mask[...] > 0).astype(F32)
    window = lax.broadcasted_iota(jnp.int32, (ROWS, WINDOW), 1)
    number = jnp.zeros((ROWS, WINDOW), F32)
    for j in range(SLOTS):
        number += jnp.where(spot[:, j : j + 1] == window, used[:, j : j + 1], 0.0)
    counts[core] = number.astype(BF16)
    count_copy = net.send(counts.at[core], counts.at[core], here.at(dc=1))

    gather_weights(here, net, (w_query, w_key, w_value), W, local_sem)

    edge_copy.wait_recv()
    hand_on = net.send(near.at[edge_here], near.at[edge_here], here.at(dc=1))
    own_copy.wait()
    pair_copy.wait_recv()
    hand_on.wait_recv()
    count_copy.wait_recv()

    @pl.loop(0, NEAR // 64)
    def _(i):
        rows = pl.ds(pl.multiple_of(i * 64, 64), 64)
        wide = near[rows, :].astype(F32)
        scale = lax.rsqrt(jnp.mean(wide * wide, axis=-1, keepdims=True) + EPSILON)
        inverse[rows, :] = jnp.broadcast_to(scale, (64, 128))
        normed[rows, :] = (wide * scale * gain[...]).astype(BF16)

    inner = pl.ds(HALO, PAIR)

    @pl.loop(0, HALF // 256)
    def _(j):
        cols = pl.ds(pl.multiple_of(j * 256, 256), 256)
        queries[:, cols] = dot(normed[inner, :], W[0, :, :, :, cols].reshape(D, 256)).astype(BF16)
        keys[:, cols] = dot(normed[...], W[1, :, :, :, cols].reshape(D, 256)).astype(BF16)
        values[:, cols] = dot(normed[...], W[2, :, :, :, cols].reshape(D, 256)).astype(BF16)

    lanes = lax.broadcasted_iota(jnp.int32, (1, 128), 1)
    low = (lanes < HEAD_DIM).astype(F32)
    low_b, high_b = low.astype(BF16), (1.0 - low).astype(BF16)
    scale = HEAD_DIM ** (-0.5)

    def two_heads(piece):
        return jnp.concatenate([piece * low_b, piece * high_b], axis=0)

    def one_piece(both):
        return jnp.where(lanes < HEAD_DIM, both[:ROWS], both[ROWS:])

    def places(i):
        block, group = i // GROUPS, i % GROUPS
        rows = pl.ds(pl.multiple_of(block * ROWS, ROWS), ROWS)
        around = pl.ds(pl.multiple_of(block * ROWS, ROWS), WINDOW)
        return block, rows, around, pl.ds(pl.multiple_of(group * 128, 128), 128)

    def count_of(block):
        one = counts[block].astype(F32)
        return jnp.concatenate([one, one], axis=0)

    @pl.loop(0, 2 * GROUPS)
    def _(i):
        block, rows, around, cols = places(i)
        number = count_of(block)
        scores = dot_nt(two_heads(queries[rows, cols]), keys[around, cols])
        weight = jnp.where(number > 0, jnp.exp(scores * scale), 0.0)
        prob = weight / jnp.sum(number * weight, axis=-1, keepdims=True)
        probs[i] = prob
        share = (prob.astype(BF16).astype(F32) * number).astype(BF16)
        mixed[rows, cols] = one_piece(dot(share, values[around, cols]))

    mine = pl.ds(pl.multiple_of(core * HALF, HALF), HALF)
    updated = (near[inner, mine].astype(F32) + mixed[...]).astype(BF16)
    reader = w_read[mine, :]
    part[...] = dot(updated, reader)
    mine_rows = pl.ds(pl.multiple_of(core * ROWS, ROWS), ROWS)
    other_rows = pl.ds(pl.multiple_of((1 - core) * ROWS, ROWS), ROWS)
    part_copy = net.send(part.at[other_rows], part_in, here.at(dc=1))
    part_copy.wait_recv()
    me = here.member
    field[me] = part[mine_rows, :] + part_in[...]

    partner = (me + X) % MEMBERS
    along = [net.send(field.at[me], field.at[me], here.at(dx=d)) for d in (1, -1, 2)]
    pieces = [pl.ds(k * 32, 32) for k in range(4)]
    over = [net.send(field.at[me, rows], field.at[me, rows], here.at(dz=8)) for rows in pieces]
    for copy, rows in zip(over, pieces):
        copy.wait_recv()
        piece = field.at[partner, rows]
        along += [net.send(piece, piece, here.at(dx=d)) for d in (1, -1, 2)]
    for copy in along:
        copy.wait_recv()

    soft = SOFTNESS * SOFTNESS
    here_field = field[me]

    def sign_of(gap):
        return gap * lax.rsqrt(gap * gap + soft)

    returned = sign_of(here_field - field[0])
    for m in range(1, MEMBERS):
        returned += sign_of(here_field - field[m])
    pulled = sign_of(here_field - target[...]) - returned / (MEMBERS - 1)
    pull[core] = pulled.astype(BF16)
    pull_copy = net.send(pull.at[core], pull.at[core], here.at(dc=1))
    pull_copy.wait_recv()
    down[...] = dot_nt(pull[...].reshape(PAIR, V), reader).astype(BF16)

    dkey[...] = jnp.zeros_like(dkey)
    dvalue[...] = jnp.zeros_like(dvalue)

    def backward(i, carry):
        block, rows, around, cols = places(i)
        number = count_of(block)
        prob = probs[i]
        given = two_heads(down[rows, cols])
        asked = two_heads(queries[rows, cols])
        share = (prob.astype(BF16).astype(F32) * number).astype(BF16)
        dprob = dot_nt(given, values[around, cols])
        level = jnp.sum(number * prob * dprob, axis=-1, keepdims=True)
        dscaled = (prob * (dprob - level) * scale).astype(BF16)
        dscaled = (dscaled.astype(F32) * number).astype(BF16)
        dquery[rows, cols] = one_piece(dot(dscaled, keys[around, cols])).astype(BF16)
        dkey[around, cols] += dot_tn(dscaled, asked)
        dvalue[around, cols] += dot_tn(share, given)
        return carry

    def send_halo(side, rows, step):
        halo_out[side, 0] = dkey[rows, :].astype(BF16)
        halo_out[side, 1] = dvalue[rows, :].astype(BF16)
        return net.send(halo_out.at[side], halo_in.at[side], here.chip(step, core))

    lax.fori_loop(0, GROUPS, backward, 0)
    to_prev = send_halo(0, pl.ds(0, HALO), -1)
    lax.fori_loop(GROUPS, 2 * GROUPS, backward, 0)
    to_next = send_halo(1, pl.ds(HALO + PAIR, HALO), 1)

    @pl.loop(0, D // 256)
    def _(j):
        cols = pl.ds(pl.multiple_of(j * 256, 256), 256)
        piece = W[0, j].reshape(256, HALF)
        back[:, cols] = dot_nt(dquery[...], piece)

    to_prev.wait_recv()
    to_next.wait_recv()
    for grad, k in ((dkey, 0), (dvalue, 1)):
        grad[pl.ds(PAIR, HALO), :] += halo_in[0, k].astype(F32)
        grad[pl.ds(HALO, HALO), :] += halo_in[1, k].astype(F32)

    @pl.loop(0, D // 256)
    def _(j):
        cols = pl.ds(pl.multiple_of(j * 256, 256), 256)
        back[:, cols] += dot_nt(dkey[inner, :].astype(BF16), W[1, j].reshape(256, HALF)) + dot_nt(
            dvalue[inner, :].astype(BF16), W[2, j].reshape(256, HALF)
        )

    back_copy = net.send(back.at[other_rows], back_in, here.at(dc=1))

    def abs_of(gap):
        return jnp.sqrt(gap * gap + soft)

    spread = jnp.full((ROWS, V), MEMBERS * SOFTNESS, F32)
    miss = jnp.zeros((ROWS, V), F32)
    for m in range(MEMBERS):
        miss += abs_of(field[m] - target[...])
        for k in range(m):
            spread += 2.0 * abs_of(field[m] - field[k])
    crps = miss / MEMBERS - spread / (2.0 * MEMBERS * (MEMBERS - 1))
    share = V // MEMBERS
    crps_out[...] = pltpu.roll(crps, (V - me * share) % V, 1)[:, :share]

    back_copy.wait_recv()

    @pl.loop(0, ROWS // 32)
    def _(i):
        rows = pl.ds(pl.multiple_of(i * 32, 32), 32)
        wide = latent[rows, :].astype(F32)
        here_rows = pl.ds(pl.multiple_of(HALO + core * ROWS + i * 32, 32), 32)
        factor = inverse[here_rows, 0:1]
        pair_rows = pl.ds(pl.multiple_of(core * ROWS + i * 32, 32), 32)
        scaled = (back[pair_rows, :] + back_in[rows, :]) * gain[...]
        fall = dot_nt(pull[core, rows, :], w_read[...])
        middle = jnp.mean(scaled * wide, axis=-1, keepdims=True)
        grad_out[rows, :] = fall + factor * scaled - wide * (factor * factor * factor * middle)

    net.drain()


def local(latent, gain, w_query, w_key, w_value, w_read, target, neighbours, slot_mask):
    vmem = pl.BlockSpec(memory_space=pltpu.VMEM)
    crps, grad = pl.pallas_call(
        body,
        out_shape=(jax.ShapeDtypeStruct((ROWS, V // MEMBERS), F32), jax.ShapeDtypeStruct((ROWS, D), F32)),
        in_specs=[vmem] * 9,
        out_specs=(vmem, vmem),
        scratch_shapes=[
            pltpu.VMEM((3, Y, Z_LO, 32, HALF), BF16),
            pltpu.VMEM((NEAR, D), BF16),
            pltpu.VMEM((NEAR, D), BF16),
            pltpu.VMEM((NEAR, 128), F32),
            pltpu.VMEM((2, ROWS, WINDOW), BF16),
            pltpu.VMEM((PAIR, HALF), BF16),
            pltpu.VMEM((NEAR, HALF), BF16),
            pltpu.VMEM((NEAR, HALF), BF16),
            pltpu.VMEM((2 * GROUPS, 2 * ROWS, WINDOW), F32),
            pltpu.VMEM((PAIR, HALF), F32),
            pltpu.VMEM((PAIR, V), F32),
            pltpu.VMEM((ROWS, V), F32),
            pltpu.VMEM((MEMBERS, ROWS, V), F32),
            pltpu.VMEM((2, ROWS, V), BF16),
            pltpu.VMEM((PAIR, HALF), BF16),
            pltpu.VMEM((PAIR, HALF), BF16),
            pltpu.VMEM((NEAR, HALF), F32),
            pltpu.VMEM((NEAR, HALF), F32),
            pltpu.VMEM((2, 2, HALO, HALF), BF16),
            pltpu.VMEM((2, 2, HALO, HALF), BF16),
            pltpu.VMEM((PAIR, D), F32),
            pltpu.VMEM((ROWS, D), F32),
            pltpu.SemaphoreType.DMA((COPIES,)),
            pltpu.SemaphoreType.DMA((COPIES,)),
            pltpu.SemaphoreType.DMA((4,)),
        ],
        compiler_params=pltpu.CompilerParams(
            collective_id=0, has_side_effects=True, vmem_limit_bytes=40 * 1024 * 1024
        ),
    )(latent[0], gain[None], w_query, w_key, w_value, w_read, target, neighbours, slot_mask)
    return crps, grad[None]


def solution(mesh):
    placed = (
        P("ens", "node", None),
        P(),
        P("node", None),
        P("node", None),
        P("node", None),
        P(),
        P("node", None),
        P("node", None),
        P("node", None),
    )
    return jax.shard_map(
        local,
        mesh=mesh,
        in_specs=placed,
        out_specs=(P("node", "ens"), P("ens", "node", None)),
        check_vma=False,
    )
```

```python
import jax
import jax.numpy as jnp
from jax import lax
from jax.experimental import pallas as pl
from jax.experimental.pallas import tpu as pltpu
from jax.sharding import PartitionSpec as P

HEAD_DIM = 64
SLOTS = 8
HALO = 64
EPSILON = 1e-06
SOFTNESS = 0.1

D = 1024
V = 128
ROWS = 128
PAIR = 2 * ROWS
NEAR = PAIR + 2 * HALO
HALF = D // 2
WINDOW = ROWS + 2 * HALO
GROUPS = HALF // 128
MEMBERS = 8
X, Y, Z, Z_LO = 4, 4, 16, 8
CHIPS = Y * Z_LO
MESH = pl.DeviceIdType.MESH
COPIES = 160
NEXT_TO = [dict(dc=1), dict(dy=1), dict(dy=-1), dict(dy=2), dict(dz=1), dict(dz=-1), dict(dx=1), dict(dx=-1), dict(dx=2)]
TELL = [[dict(dz=1), dict(dz=-1)], [dict(dz=2), dict(dz=-2)], [dict(dz=4), dict(dz=-4)], [dict(dy=1), dict(dy=-1)]]

F32 = jnp.float32
BF16 = jnp.bfloat16
NT = (((1,), (1,)), ((), ()))
TN = (((0,), (0,)), ((), ()))


def dot(a, b):
    return jnp.dot(a, b, preferred_element_type=F32)


def dot_nt(a, b):
    return lax.dot_general(a, b, NT, preferred_element_type=F32)


def dot_tn(a, b):
    return lax.dot_general(a, b, TN, preferred_element_type=F32)


class Place:
    def __init__(self):
        self.member = lax.axis_index("ens")
        self.node = lax.axis_index("node")
        self.x = self.member % X
        self.y = self.node // (2 * Z_LO)
        self.z = (self.member // X) * Z_LO + (self.node // 2) % Z_LO
        self.core = self.node % 2

    def at(self, dx=0, dy=0, dz=0, dc=0):
        x, y, z = (self.x + dx + X) % X, (self.y + dy + Y) % Y, (self.z + dz + Z) % Z
        core = (self.core + dc) % 2
        return {"ens": (z // Z_LO) * X + x, "node": (y * Z_LO + z % Z_LO) * 2 + core}

    def chip(self, step, core):
        return {"ens": self.member, "node": ((self.node // 2 + step + CHIPS) % CHIPS) * 2 + core}


class Net:
    def __init__(self, send_sem, recv_sem):
        self.send_sem, self.recv_sem = send_sem, recv_sem
        self.count = 0
        self.sent = []

    def send(self, src, dst, to):
        copy = pltpu.make_async_remote_copy(
            src_ref=src,
            dst_ref=dst,
            send_sem=self.send_sem.at[self.count],
            recv_sem=self.recv_sem.at[self.count],
            device_id=to,
            device_id_type=MESH,
        )
        self.count += 1
        copy.start()
        self.sent.append(copy)
        return copy

    def drain(self):
        for copy in self.sent:
            copy.wait_send()


def gather_weights(here, net, w_refs, W, local_sem, between):
    y, z, c = here.y, here.z % Z_LO, here.core
    mine, other = pl.multiple_of(c * HALF, HALF), pl.multiple_of((1 - c) * HALF, HALF)
    own_rows = pl.ds(pl.multiple_of(c * 16, 16), 16)
    local, swap = [], []
    for i, w in enumerate(w_refs):
        spot = W.at[i, y, z, own_rows]
        swap.append(net.send(w.at[:, pl.ds(other, HALF)], spot, here.at(dc=1)))
        local.append(pltpu.make_async_copy(w.at[:, pl.ds(mine, HALF)], spot, local_sem.at[i]))
        local[-1].start()
    for copy in local:
        copy.wait()
    for copy in swap:
        copy.wait_recv()

    first, second = pl.ds(0, 16), pl.ds(16, 16)
    kept = pl.ds(here.x % 2, 2)
    given = (here.x % 2) * 2
    across = []

    def pass_on(rows, ys, zs):
        piece = W.at[given, ys, zs, rows]
        across.append(net.send(piece, piece, here.at(dx=1 if rows is first else -1)))

    def forward(ys, zs, rows, **step):
        piece = W.at[kept, ys, zs, rows]
        return net.send(piece, piece, here.at(**step))

    every = slice(None)
    below, above, far = (y + 3) % Y, (y + 1) % Y, (y + 2) % Y
    along_y = [forward(y, z, first, dy=d) for d in (1, -1, 2)]
    second_up, second_down = forward(y, z, second, dz=1), forward(y, z, second, dz=-1)
    pending = [(z, forward(y, z, second, dy=1), forward(y, z, second, dy=-1))]
    between[0]()
    for copy in along_y:
        copy.wait_recv()
    first_up, first_down = forward(every, z, first, dz=1), forward(every, z, first, dz=-1)
    for ys in (below, above, far):
        pass_on(first, ys, z)
    relayed = []

    def spread(zs, from_below, from_above):
        from_below.wait_recv()
        from_above.wait_recv()
        if len(relayed) % 2 == 0:
            relayed.append((zs, forward(below, zs, second, dy=1)))
        else:
            relayed.append((zs, forward(above, zs, second, dy=-1)))
        for ys in (below, above) if zs is z else (below, above, y):
            pass_on(second, ys, zs)

    last = Z_LO // 2
    for step in range(1, last + 1):
        before, after = (z + Z_LO - step) % Z_LO, (z + step) % Z_LO
        arrived = []
        if step < last:
            second_up.wait_recv()
            if step < last - 1:
                second_up = forward(y, before, second, dz=1)
            arrived.append((before, forward(y, before, second, dy=1), forward(y, before, second, dy=-1)))
        second_down.wait_recv()
        if step < last:
            second_down = forward(y, after, second, dz=-1)
        arrived.append((after, forward(y, after, second, dy=1), forward(y, after, second, dy=-1)))
        first_up.wait_recv()
        first_down.wait_recv()
        if step < last - 1:
            first_up, first_down = forward(every, before, first, dz=1), forward(every, after, first, dz=-1)
        elif step == last - 1:
            first_up = forward(pl.ds(0, 2), before, first, dz=1)
            first_down = forward(pl.ds(2, 2), after, first, dz=-1)
        if step < last:
            pass_on(first, every, before)
        pass_on(first, every, after)
        for item in pending:
            spread(*item)
        pending = arrived
        between[step]()
    for item in pending:
        spread(*item)
    between[last + 1]()
    for zs, copy in relayed:
        copy.wait_recv()
        pass_on(second, far, zs)
    between[last + 2]()
    for copy in across:
        copy.wait_recv()


def body(
    latent, gain_in, w_query, w_key, w_value, w_read_in, target_in, neighbours, slot_mask,
    crps_out, grad_out,
    gain, w_read, target, slots,
    W, near, normed, inverse, counts, queries, keys, values, probs, mixed,
    part, part_in, field, pull, down, dquery, dkey, dvalue, halo_out, halo_in, back, back_in,
    send_sem, recv_sem, local_sem, input_sem, ready,
):
    here = Place()
    net = Net(send_sem, recv_sem)
    core = here.core
    inputs = [(gain_in, gain), (w_read_in, w_read), (target_in, target), (neighbours, slots.at[0]), (slot_mask, slots.at[1])]
    inputs = [pltpu.make_async_copy(src, dst, input_sem.at[i]) for i, (src, dst) in enumerate(inputs)]
    peers = [here.at(**step) for step in NEXT_TO]
    barrier = pltpu.get_barrier_semaphore()
    for peer in peers:
        pl.semaphore_signal(barrier, inc=1, device_id=peer, device_id_type=MESH)
    for copy in inputs:
        copy.start()
    pl.semaphore_wait(barrier, len(peers))

    own = pl.ds(pl.multiple_of(HALO + core * ROWS, 64), ROWS)
    edge = pl.ds(pl.multiple_of(core * HALO, 64), HALO)
    edge_there = pl.ds(pl.multiple_of((1 - core) * (HALO + PAIR), 64), HALO)
    edge_here = pl.ds(pl.multiple_of(core * (HALO + PAIR), 64), HALO)
    own_copy = pltpu.make_async_copy(latent, near.at[own], local_sem.at[3])
    copies = {}

    def tell(step):
        for to in TELL[step]:
            pl.semaphore_signal(ready.at[step], inc=1, device_id=here.at(**to), device_id_type=MESH)

    def hear(step):
        pl.semaphore_wait(ready.at[step], len(TELL[step]))

    def normalize(start, count):
        @pl.loop(0, count // 64)
        def _(i):
            rows = pl.ds(pl.multiple_of(start + i * 64, 64), 64)
            wide = near[rows, :].astype(F32)
            scale = lax.rsqrt(jnp.mean(wide * wide, axis=-1, keepdims=True) + EPSILON)
            inverse[rows, :] = jnp.broadcast_to(scale, (64, 128))
            normed[rows, :] = (wide * scale * gain[...]).astype(BF16)

    def count_slots():
        for copy in inputs:
            copy.wait()
        first = here.node * ROWS - HALO
        total = 2 * CHIPS * ROWS
        spot = slots[0] - first
        spot = jnp.where(spot < 0, spot + total, spot)
        spot = jnp.where(spot >= total, spot - total, spot)
        spot = jnp.where(slots[1] > 0, spot, -1).astype(F32).T
        window = lax.broadcasted_iota(jnp.int32, (ROWS, WINDOW), 1).astype(F32)
        number = jnp.zeros((ROWS, WINDOW), F32)
        for j in range(SLOTS):
            number += jnp.where(spot[:, j : j + 1] == window, 1.0, 0.0)
        counts[core] = number.astype(BF16)
        copies["count"] = net.send(counts.at[core], counts.at[core], here.at(dc=1))

    def between_0():
        own_copy.start()
        copies["pair"] = net.send(latent, near.at[own], here.at(dc=1))
        tell(0)
        count_slots()
        hear(0)
        tell(1)

    def between_1():
        hear(1)
        tell(2)
        own_copy.wait()
        normalize(HALO + core * ROWS, ROWS)

    def between_2():
        hear(2)
        tell(3)
        copies["pair"].wait_recv()
        normalize(HALO + (1 - core) * ROWS, ROWS)

    def between_3():
        hear(3)
        copies["edge"] = net.send(latent.at[edge], near.at[edge_there], here.chip(2 * core - 1, 1 - core))

    def between_5():
        copies["edge"].wait_recv()
        copies["hand_on"] = net.send(near.at[edge_here], near.at[edge_here], here.at(dc=1))
        normalize(core * (HALO + PAIR), HALO)

    def between_6():
        copies["hand_on"].wait_recv()
        normalize((1 - core) * (HALO + PAIR), HALO)
        copies["count"].wait_recv()

    between = [between_0, between_1, between_2, between_3, lambda: None, between_5, between_6]
    gather_weights(here, net, (w_query, w_key, w_value), W, local_sem, between)

    inner = pl.ds(HALO, PAIR)

    @pl.loop(0, HALF // 256)
    def _(j):
        cols = pl.ds(pl.multiple_of(j * 256, 256), 256)
        queries[:, cols] = dot(normed[inner, :], W[0, :, :, :, cols].reshape(D, 256)).astype(BF16)
        keys[:, cols] = dot(normed[...], W[1, :, :, :, cols].reshape(D, 256)).astype(BF16)
        values[:, cols] = dot(normed[...], W[2, :, :, :, cols].reshape(D, 256)).astype(BF16)

    lanes = lax.broadcasted_iota(jnp.int32, (1, 128), 1)
    low = (lanes < HEAD_DIM).astype(F32)
    low_b, high_b = low.astype(BF16), (1.0 - low).astype(BF16)
    scale = HEAD_DIM ** (-0.5)

    def two_heads(piece):
        return jnp.concatenate([piece * low_b, piece * high_b], axis=0)

    def one_piece(both):
        return jnp.where(lanes < HEAD_DIM, both[:ROWS], both[ROWS:])

    def places(i):
        block, group = i // GROUPS, i % GROUPS
        rows = pl.ds(pl.multiple_of(block * ROWS, ROWS), ROWS)
        around = pl.ds(pl.multiple_of(block * ROWS, ROWS), WINDOW)
        return block, rows, around, pl.ds(pl.multiple_of(group * 128, 128), 128)

    def count_of(block):
        one = counts[block].astype(F32)
        return jnp.concatenate([one, one], axis=0)

    @pl.loop(0, 2 * GROUPS)
    def _(i):
        block, rows, around, cols = places(i)
        number = count_of(block)
        scores = dot_nt(two_heads(queries[rows, cols]), keys[around, cols])
        weight = jnp.where(number > 0, jnp.exp(scores * scale), 0.0)
        prob = weight / jnp.sum(number * weight, axis=-1, keepdims=True)
        probs[i] = prob
        share = (prob.astype(BF16).astype(F32) * number).astype(BF16)
        mixed[rows, cols] = one_piece(dot(share, values[around, cols]))

    mine = pl.ds(pl.multiple_of(core * HALF, HALF), HALF)
    updated = (near[inner, mine].astype(F32) + mixed[...]).astype(BF16)
    reader = w_read[mine, :]
    part[...] = dot(updated, reader)
    mine_rows = pl.ds(pl.multiple_of(core * ROWS, ROWS), ROWS)
    other_rows = pl.ds(pl.multiple_of((1 - core) * ROWS, ROWS), ROWS)
    part_copy = net.send(part.at[other_rows], part_in, here.at(dc=1))
    part_copy.wait_recv()
    me = here.member
    field[me] = part[mine_rows, :] + part_in[...]

    partner = (me + X) % MEMBERS
    along = [net.send(field.at[me], field.at[me], here.at(dx=d)) for d in (1, -1, 2)]
    pieces = [pl.ds(k * 32, 32) for k in range(4)]
    over = [net.send(field.at[me, rows], field.at[me, rows], here.at(dz=8)) for rows in pieces]
    for copy, rows in zip(over, pieces):
        copy.wait_recv()
        piece = field.at[partner, rows]
        along += [net.send(piece, piece, here.at(dx=d)) for d in (1, -1, 2)]
    for copy in along:
        copy.wait_recv()

    soft = SOFTNESS * SOFTNESS
    here_field = field[me]

    def sign_of(gap):
        return gap * lax.rsqrt(gap * gap + soft)

    returned = sign_of(here_field - field[0])
    for m in range(1, MEMBERS):
        returned += sign_of(here_field - field[m])
    pulled = sign_of(here_field - target[...]) - returned / (MEMBERS - 1)
    pull[core] = pulled.astype(BF16)
    pull_copy = net.send(pull.at[core], pull.at[core], here.at(dc=1))
    pull_copy.wait_recv()
    down[...] = dot_nt(pull[...].reshape(PAIR, V), reader).astype(BF16)

    dkey[...] = jnp.zeros_like(dkey)
    dvalue[...] = jnp.zeros_like(dvalue)

    def backward(i, carry):
        block, rows, around, cols = places(i)
        number = count_of(block)
        prob = probs[i]
        given = two_heads(down[rows, cols])
        asked = two_heads(queries[rows, cols])
        share = (prob.astype(BF16).astype(F32) * number).astype(BF16)
        dprob = dot_nt(given, values[around, cols])
        level = jnp.sum(number * prob * dprob, axis=-1, keepdims=True)
        dscaled = (prob * (dprob - level) * scale).astype(BF16)
        dscaled = (dscaled.astype(F32) * number).astype(BF16)
        dquery[rows, cols] = one_piece(dot(dscaled, keys[around, cols])).astype(BF16)
        dkey[around, cols] += dot_tn(dscaled, asked)
        dvalue[around, cols] += dot_tn(share, given)
        return carry

    def send_halo(side, rows, step):
        halo_out[side, 0] = dkey[rows, :].astype(BF16)
        halo_out[side, 1] = dvalue[rows, :].astype(BF16)
        return net.send(halo_out.at[side], halo_in.at[side], here.chip(step, core))

    lax.fori_loop(0, GROUPS, backward, 0)
    to_prev = send_halo(0, pl.ds(0, HALO), -1)
    lax.fori_loop(GROUPS, 2 * GROUPS, backward, 0)
    to_next = send_halo(1, pl.ds(HALO + PAIR, HALO), 1)

    @pl.loop(0, D // 256)
    def _(j):
        cols = pl.ds(pl.multiple_of(j * 256, 256), 256)
        piece = W[0, j].reshape(256, HALF)
        back[:, cols] = dot_nt(dquery[...], piece)

    def abs_of(gap):
        return jnp.sqrt(gap * gap + soft)

    spread = jnp.full((ROWS, V), MEMBERS * SOFTNESS, F32)
    miss = jnp.zeros((ROWS, V), F32)
    for m in range(MEMBERS):
        miss += abs_of(field[m] - target[...])
        for k in range(m):
            spread += 2.0 * abs_of(field[m] - field[k])
    crps = miss / MEMBERS - spread / (2.0 * MEMBERS * (MEMBERS - 1))
    share = V // MEMBERS
    crps_out[...] = pltpu.roll(crps, (V - me * share) % V, 1).T[:share, :]

    to_prev.wait_recv()
    to_next.wait_recv()
    for grad, k in ((dkey, 0), (dvalue, 1)):
        grad[pl.ds(PAIR, HALO), :] += halo_in[0, k].astype(F32)
        grad[pl.ds(HALO, HALO), :] += halo_in[1, k].astype(F32)

    @pl.loop(0, D // 256)
    def _(j):
        cols = pl.ds(pl.multiple_of(j * 256, 256), 256)
        back[:, cols] += dot_nt(dkey[inner, :].astype(BF16), W[1, j].reshape(256, HALF)) + dot_nt(
            dvalue[inner, :].astype(BF16), W[2, j].reshape(256, HALF)
        )

    back_copy = net.send(back.at[other_rows], back_in, here.at(dc=1))

    back_copy.wait_recv()

    @pl.loop(0, ROWS // 32)
    def _(i):
        rows = pl.ds(pl.multiple_of(i * 32, 32), 32)
        here_rows = pl.ds(pl.multiple_of(HALO + core * ROWS + i * 32, 32), 32)
        wide = near[here_rows, :].astype(F32)
        factor = inverse[here_rows, 0:1]
        pair_rows = pl.ds(pl.multiple_of(core * ROWS + i * 32, 32), 32)
        scaled = (back[pair_rows, :] + back_in[rows, :]) * gain[...]
        fall = dot_nt(pull[core, rows, :], w_read[...])
        middle = jnp.mean(scaled * wide, axis=-1, keepdims=True)
        grad_out[rows, :] = fall + factor * scaled - wide * (factor * factor * factor * middle)

    net.drain()


def local(latent, gain, w_query, w_key, w_value, w_read, target, neighbours, slot_mask):
    vmem, hbm = pl.BlockSpec(memory_space=pltpu.VMEM), pl.BlockSpec(memory_space=pltpu.HBM)
    crps, grad = pl.pallas_call(
        body,
        out_shape=(jax.ShapeDtypeStruct((V // MEMBERS, ROWS), F32), jax.ShapeDtypeStruct((ROWS, D), F32)),
        in_specs=[hbm] * 9,
        out_specs=(vmem, vmem),
        scratch_shapes=[
            pltpu.VMEM((1, D), F32),
            pltpu.VMEM((D, V), BF16),
            pltpu.VMEM((ROWS, V), F32),
            pltpu.VMEM((2, SLOTS, ROWS), jnp.int32),
            pltpu.VMEM((3, Y, Z_LO, 32, HALF), BF16),
            pltpu.VMEM((NEAR, D), BF16),
            pltpu.VMEM((NEAR, D), BF16),
            pltpu.VMEM((NEAR, 128), F32),
            pltpu.VMEM((2, ROWS, WINDOW), BF16),
            pltpu.VMEM((PAIR, HALF), BF16),
            pltpu.VMEM((NEAR, HALF), BF16),
            pltpu.VMEM((NEAR, HALF), BF16),
            pltpu.VMEM((2 * GROUPS, 2 * ROWS, WINDOW), F32),
            pltpu.VMEM((PAIR, HALF), F32),
            pltpu.VMEM((PAIR, V), F32),
            pltpu.VMEM((ROWS, V), F32),
            pltpu.VMEM((MEMBERS, ROWS, V), F32),
            pltpu.VMEM((2, ROWS, V), BF16),
            pltpu.VMEM((PAIR, HALF), BF16),
            pltpu.VMEM((PAIR, HALF), BF16),
            pltpu.VMEM((NEAR, HALF), F32),
            pltpu.VMEM((NEAR, HALF), F32),
            pltpu.VMEM((2, 2, HALO, HALF), BF16),
            pltpu.VMEM((2, 2, HALO, HALF), BF16),
            pltpu.VMEM((PAIR, D), F32),
            pltpu.VMEM((ROWS, D), F32),
            pltpu.SemaphoreType.DMA((COPIES,)),
            pltpu.SemaphoreType.DMA((COPIES,)),
            pltpu.SemaphoreType.DMA((4,)),
            pltpu.SemaphoreType.DMA((5,)),
            pltpu.SemaphoreType.REGULAR((len(TELL),)),
        ],
        compiler_params=pltpu.CompilerParams(
            collective_id=0, has_side_effects=True, vmem_limit_bytes=63 * 1024 * 1024
        ),
    )(latent[0], gain[None], w_query, w_key, w_value, w_read, target, neighbours.T, slot_mask.T)
    return crps.T, grad[None]


def solution(mesh):
    placed = (
        P("ens", "node", None),
        P(),
        P("node", None),
        P("node", None),
        P("node", None),
        P(),
        P("node", None),
        P("node", None),
        P("node", None),
    )
    return jax.shard_map(
        local,
        mesh=mesh,
        in_specs=placed,
        out_specs=(P("node", "ens"), P("ens", "node", None)),
        check_vma=False,
    )
```

```python
import jax
import jax.numpy as jnp
from jax import lax
from jax.experimental import pallas as pl
from jax.experimental.pallas import tpu as pltpu
from jax.sharding import PartitionSpec as P

HEAD_DIM = 64
SLOTS = 8
HALO = 64
EPSILON = 1e-06
SOFTNESS = 0.1

D = 1024
V = 128
ROWS = 128
PAIR = 2 * ROWS
NEAR = PAIR + 2 * HALO
HALF = D // 2
WINDOW = ROWS + 2 * HALO
GROUPS = HALF // 128
MEMBERS = 8
X, Y, Z, Z_LO = 4, 4, 16, 8
CHIPS = Y * Z_LO
MESH = pl.DeviceIdType.MESH
COPIES = 160
NEXT_TO = [dict(dc=1), dict(dy=1), dict(dy=-1), dict(dy=2), dict(dz=1), dict(dz=-1), dict(dx=1), dict(dx=-1), dict(dx=2)]
TELL = [[dict(dz=1), dict(dz=-1)], [dict(dz=2), dict(dz=-2)], [dict(dz=4), dict(dz=-4)], [dict(dy=1), dict(dy=-1)]]

F32 = jnp.float32
BF16 = jnp.bfloat16
NT = (((1,), (1,)), ((), ()))
TN = (((0,), (0,)), ((), ()))


def dot(a, b):
    return jnp.dot(a, b, preferred_element_type=F32)


def dot_nt(a, b):
    return lax.dot_general(a, b, NT, preferred_element_type=F32)


def dot_tn(a, b):
    return lax.dot_general(a, b, TN, preferred_element_type=F32)


class Place:
    def __init__(self):
        self.member = lax.axis_index("ens")
        self.node = lax.axis_index("node")
        self.x = self.member % X
        self.y = self.node // (2 * Z_LO)
        self.z = (self.member // X) * Z_LO + (self.node // 2) % Z_LO
        self.core = self.node % 2

    def at(self, dx=0, dy=0, dz=0, dc=0):
        x, y, z = (self.x + dx + X) % X, (self.y + dy + Y) % Y, (self.z + dz + Z) % Z
        core = (self.core + dc) % 2
        return {"ens": (z // Z_LO) * X + x, "node": (y * Z_LO + z % Z_LO) * 2 + core}

    def chip(self, step, core):
        return {"ens": self.member, "node": ((self.node // 2 + step + CHIPS) % CHIPS) * 2 + core}


class Net:
    def __init__(self, send_sem, recv_sem):
        self.send_sem, self.recv_sem = send_sem, recv_sem
        self.count = 0
        self.sent = []

    def send(self, src, dst, to):
        copy = pltpu.make_async_remote_copy(
            src_ref=src,
            dst_ref=dst,
            send_sem=self.send_sem.at[self.count],
            recv_sem=self.recv_sem.at[self.count],
            device_id=to,
            device_id_type=MESH,
        )
        self.count += 1
        copy.start()
        self.sent.append(copy)
        return copy

    def drain(self):
        for copy in self.sent:
            copy.wait_send()


def gather_weights(here, net, w_refs, W, local_sem, between):
    y, z, c = here.y, here.z % Z_LO, here.core
    mine, other = pl.multiple_of(c * HALF, HALF), pl.multiple_of((1 - c) * HALF, HALF)
    own_rows = pl.ds(pl.multiple_of(c * 16, 16), 16)
    local, swap = [], []
    for i, w in enumerate(w_refs):
        spot = W.at[i, y, z, own_rows]
        swap.append(net.send(w.at[:, pl.ds(other, HALF)], spot, here.at(dc=1)))
        local.append(pltpu.make_async_copy(w.at[:, pl.ds(mine, HALF)], spot, local_sem.at[i]))
        local[-1].start()
    for copy in local:
        copy.wait()
    for copy in swap:
        copy.wait_recv()

    first, second = pl.ds(0, 16), pl.ds(16, 16)
    kept = pl.ds(here.x % 2, 2)
    given = (here.x % 2) * 2
    across = []

    def pass_on(rows, ys, zs):
        piece = W.at[given, ys, zs, rows]
        across.append(net.send(piece, piece, here.at(dx=1 if rows is first else -1)))

    def forward(ys, zs, rows, **step):
        piece = W.at[kept, ys, zs, rows]
        return net.send(piece, piece, here.at(**step))

    every = slice(None)
    below, above, far = (y + 3) % Y, (y + 1) % Y, (y + 2) % Y
    def spread(zs):
        return (zs, [forward(y, zs, second, dy=d) for d in (1, -1, 2)])

    def settle(zs, copies):
        for copy in copies:
            copy.wait_recv()
        for ys in (below, above, far) if zs is z else (below, above, far, y):
            pass_on(second, ys, zs)

    def forward_first(piece, zs, **step):
        k, ys = piece
        part = W.at[here.x % 2 + k, ys, zs, first]
        return net.send(part, part, here.at(**step))

    second_up, second_down = forward(y, z, second, dz=1), forward(y, z, second, dz=-1)
    along_y = [forward(y, z, first, dy=d) for d in (1, -1, 2)]
    pending = [spread(z)]
    between[0]()
    for copy in along_y:
        copy.wait_recv()
    pieces = [(k, pl.ds(2 * j, 2)) for j in range(2) for k in range(2)]
    up = [forward_first(piece, z, dz=1) for piece in pieces]
    down = [forward_first(piece, z, dz=-1) for piece in pieces]
    for ys in (below, above, far):
        pass_on(first, ys, z)

    last = Z_LO // 2
    for step in range(1, last + 1):
        before, after = (z + Z_LO - step) % Z_LO, (z + step) % Z_LO
        arrived = []
        if step < last:
            second_up.wait_recv()
            if step < last - 1:
                second_up = forward(y, before, second, dz=1)
        second_down.wait_recv()
        if step < last:
            second_down = forward(y, after, second, dz=-1)
            arrived.append(spread(before))
        arrived.append(spread(after))
        if step < last:
            next_up, next_down = [], []
            for i, piece in enumerate(pieces):
                up[i].wait_recv()
                if step < last - 1 or i < 2:
                    next_up.append(forward_first(piece, before, dz=1))
                down[i].wait_recv()
                if step < last - 1 or i >= 2:
                    next_down.append(forward_first(piece, after, dz=-1))
            up, down = next_up, next_down
            pass_on(first, every, before)
            pass_on(first, every, after)
        else:
            for copy in up + down:
                copy.wait_recv()
            pass_on(first, every, after)
        for item in pending:
            settle(*item)
        pending = arrived
        between[step]()
    for item in pending:
        settle(*item)
    between[last + 1]()
    between[last + 2]()
    for copy in across:
        copy.wait_recv()


def body(
    latent, gain_in, w_query, w_key, w_value, w_read_in, target_in, neighbours, slot_mask,
    crps_out, grad_out,
    gain, w_read, target, slots,
    W, near, normed, inverse, counts, queries, keys, values, probs, mixed,
    part, part_in, field, pull, down, dquery, dkey, dvalue, halo_out, halo_in, back, back_in,
    send_sem, recv_sem, local_sem, input_sem, ready,
):
    here = Place()
    net = Net(send_sem, recv_sem)
    core = here.core
    inputs = [(gain_in, gain), (w_read_in, w_read), (target_in, target), (neighbours, slots.at[0]), (slot_mask, slots.at[1])]
    inputs = [pltpu.make_async_copy(src, dst, input_sem.at[i]) for i, (src, dst) in enumerate(inputs)]
    peers = [here.at(**step) for step in NEXT_TO]
    barrier = pltpu.get_barrier_semaphore()
    for peer in peers:
        pl.semaphore_signal(barrier, inc=1, device_id=peer, device_id_type=MESH)
    for copy in inputs:
        copy.start()
    pl.semaphore_wait(barrier, len(peers))

    own = pl.ds(pl.multiple_of(HALO + core * ROWS, 64), ROWS)
    edge = pl.ds(pl.multiple_of(core * HALO, 64), HALO)
    edge_there = pl.ds(pl.multiple_of((1 - core) * (HALO + PAIR), 64), HALO)
    edge_here = pl.ds(pl.multiple_of(core * (HALO + PAIR), 64), HALO)
    own_copy = pltpu.make_async_copy(latent, near.at[own], local_sem.at[3])
    copies = {}

    def tell(step):
        for to in TELL[step]:
            pl.semaphore_signal(ready.at[step], inc=1, device_id=here.at(**to), device_id_type=MESH)

    def hear(step):
        pl.semaphore_wait(ready.at[step], len(TELL[step]))

    def normalize(start, count):
        @pl.loop(0, count // 64)
        def _(i):
            rows = pl.ds(pl.multiple_of(start + i * 64, 64), 64)
            wide = near[rows, :].astype(F32)
            scale = lax.rsqrt(jnp.mean(wide * wide, axis=-1, keepdims=True) + EPSILON)
            inverse[rows, :] = jnp.broadcast_to(scale, (64, 128))
            normed[rows, :] = (wide * scale * gain[...]).astype(BF16)

    def count_slots():
        for copy in inputs:
            copy.wait()
        first = here.node * ROWS - HALO
        total = 2 * CHIPS * ROWS
        spot = slots[0] - first
        spot = jnp.where(spot < 0, spot + total, spot)
        spot = jnp.where(spot >= total, spot - total, spot)
        spot = jnp.where(slots[1] > 0, spot, -1).astype(F32).T
        window = lax.broadcasted_iota(jnp.int32, (ROWS, WINDOW), 1).astype(F32)
        number = jnp.zeros((ROWS, WINDOW), F32)
        for j in range(SLOTS):
            number += jnp.where(spot[:, j : j + 1] == window, 1.0, 0.0)
        counts[core] = number.astype(BF16)
        copies["count"] = net.send(counts.at[core], counts.at[core], here.at(dc=1))

    def between_0():
        own_copy.start()
        copies["pair"] = net.send(latent, near.at[own], here.at(dc=1))
        tell(0)
        count_slots()
        hear(0)
        tell(1)

    def between_1():
        hear(1)
        tell(2)
        own_copy.wait()
        normalize(HALO + core * ROWS, ROWS)

    def between_2():
        hear(2)
        tell(3)
        copies["pair"].wait_recv()
        normalize(HALO + (1 - core) * ROWS, ROWS)

    def between_3():
        hear(3)
        copies["edge"] = net.send(latent.at[edge], near.at[edge_there], here.chip(2 * core - 1, 1 - core))

    def between_5():
        copies["edge"].wait_recv()
        copies["hand_on"] = net.send(near.at[edge_here], near.at[edge_here], here.at(dc=1))
        normalize(core * (HALO + PAIR), HALO)

    def between_6():
        copies["hand_on"].wait_recv()
        normalize((1 - core) * (HALO + PAIR), HALO)
        copies["count"].wait_recv()

    between = [between_0, between_1, between_2, between_3, lambda: None, between_5, between_6]
    gather_weights(here, net, (w_query, w_key, w_value), W, local_sem, between)

    inner = pl.ds(HALO, PAIR)

    @pl.loop(0, HALF // 256)
    def _(j):
        cols = pl.ds(pl.multiple_of(j * 256, 256), 256)
        queries[:, cols] = dot(normed[inner, :], W[0, :, :, :, cols].reshape(D, 256)).astype(BF16)
        keys[:, cols] = dot(normed[...], W[1, :, :, :, cols].reshape(D, 256)).astype(BF16)
        values[:, cols] = dot(normed[...], W[2, :, :, :, cols].reshape(D, 256)).astype(BF16)

    lanes = lax.broadcasted_iota(jnp.int32, (1, 128), 1)
    low = (lanes < HEAD_DIM).astype(F32)
    low_b, high_b = low.astype(BF16), (1.0 - low).astype(BF16)
    scale = HEAD_DIM ** (-0.5)

    def two_heads(piece):
        return jnp.concatenate([piece * low_b, piece * high_b], axis=0)

    def one_piece(both):
        return jnp.where(lanes < HEAD_DIM, both[:HALO], both[HALO:])

    def start_of(half, block):
        return block * ROWS + HALO * ((half + block) % 2)

    def places(half, block, group):
        rows = pl.ds(start_of(half, block), HALO)
        around = pl.ds(block * ROWS, WINDOW)
        return rows, around, pl.ds(pl.multiple_of(group * 128, 128), 128)

    def count_of(half, block):
        one = counts[block, pl.ds(HALO * ((half + block) % 2), HALO), :].astype(F32)
        return jnp.concatenate([one, one], axis=0)

    mine = pl.ds(pl.multiple_of(core * HALF, HALF), HALF)
    me = here.member
    partner = (me + X) % MEMBERS
    fields = [{}, {}]

    def own_rows(half, offset=0, count=HALO):
        return pl.ds(pl.multiple_of(HALO * ((half + core) % 2) + offset, 32), count)

    def attend(half):
        @pl.loop(0, GROUPS)
        def _(group):
            for block in range(2):
                rows, around, cols = places(half, block, group)
                number = count_of(half, block)
                scores = dot_nt(two_heads(queries[rows, cols]), keys[around, cols])
                weight = jnp.where(number > 0, jnp.exp(scores * scale), 0.0)
                prob = weight / jnp.sum(number * weight, axis=-1, keepdims=True)
                probs[half, block, group] = prob
                share = (prob.astype(BF16).astype(F32) * number).astype(BF16)
                mixed[rows, cols] = one_piece(dot(share, values[around, cols]))

    def read_out(half):
        for block in range(2):
            rows = pl.ds(start_of(half, block), HALO)
            wide = near[pl.ds(HALO + start_of(half, block), HALO), mine].astype(F32)
            part[rows, :] = dot((wide + mixed[rows, :]).astype(BF16), w_read[mine, :])
        theirs = pl.ds(pl.multiple_of((1 - core) * ROWS + HALO * ((half + 1 - core) % 2), 64), HALO)
        ours = pl.ds(pl.multiple_of(core * ROWS + HALO * ((half + core) % 2), 64), HALO)
        net.send(part.at[theirs], part_in.at[half], here.at(dc=1)).wait_recv()
        field[me, own_rows(half), :] = part[ours, :] + part_in[half]
        pieces = [field.at[me, own_rows(half, 32 * k, 32)] for k in range(2)]
        fields[half]["over"] = [net.send(piece, piece, here.at(dz=8)) for piece in pieces]
        whole = field.at[me, own_rows(half)]
        fields[half]["along"] = [net.send(whole, whole, here.at(dx=d)) for d in (1, -1, 2)]

    def relay(half):
        for k, copy in enumerate(fields[half]["over"]):
            copy.wait_recv()
            piece = field.at[partner, own_rows(half, 32 * k, 32)]
            fields[half]["along"] += [net.send(piece, piece, here.at(dx=d)) for d in (1, -1, 2)]

    soft = SOFTNESS * SOFTNESS

    def sign_of(gap):
        return gap * lax.rsqrt(gap * gap + soft)

    def pull_back(half):
        for copy in fields[half]["along"]:
            copy.wait_recv()
        rows = own_rows(half)
        here_field = field[me, rows, :]
        returned = sign_of(here_field - field[0, rows, :])
        for m in range(1, MEMBERS):
            returned += sign_of(here_field - field[m, rows, :])
        pulled = sign_of(here_field - target[rows, :]) - returned / (MEMBERS - 1)
        pull[core, rows, :] = pulled.astype(BF16)
        piece = pull.at[core, rows]
        net.send(piece, piece, here.at(dc=1)).wait_recv()
        for block in range(2):
            there = pull[block, pl.ds(HALO * ((half + block) % 2), HALO), :]
            down[pl.ds(start_of(half, block), HALO), :] = dot_nt(there, w_read[mine, :]).astype(BF16)

    def backward(half):
        @pl.loop(0, GROUPS)
        def _(group):
            for block in range(2):
                rows, around, cols = places(half, block, group)
                number = count_of(half, block)
                prob = probs[half, block, group]
                given = two_heads(down[rows, cols])
                asked = two_heads(queries[rows, cols])
                share = (prob.astype(BF16).astype(F32) * number).astype(BF16)
                dprob = dot_nt(given, values[around, cols])
                level = jnp.sum(number * prob * dprob, axis=-1, keepdims=True)
                dscaled = (prob * (dprob - level) * scale).astype(BF16)
                dscaled = (dscaled.astype(F32) * number).astype(BF16)
                dquery[rows, cols] = one_piece(dot(dscaled, keys[around, cols])).astype(BF16)
                dkey[around, cols] += dot_tn(dscaled, asked)
                dvalue[around, cols] += dot_tn(share, given)

    def send_halo(side, rows, step):
        halo_out[side, 0] = dkey[rows, :].astype(BF16)
        halo_out[side, 1] = dvalue[rows, :].astype(BF16)
        return net.send(halo_out.at[side], halo_in.at[side], here.chip(step, core))

    for half in range(2):
        attend(half)
        read_out(half)
    dkey[...] = jnp.zeros_like(dkey)
    dvalue[...] = jnp.zeros_like(dvalue)
    relay(0)
    relay(1)
    pull_back(0)
    backward(0)
    to_prev = send_halo(0, pl.ds(0, HALO), -1)
    to_next = send_halo(1, pl.ds(HALO + PAIR, HALO), 1)
    pull_back(1)
    backward(1)

    mine_rows = pl.ds(pl.multiple_of(core * ROWS, ROWS), ROWS)
    other_rows = pl.ds(pl.multiple_of((1 - core) * ROWS, ROWS), ROWS)

    @pl.loop(0, D // 256)
    def _(j):
        cols = pl.ds(pl.multiple_of(j * 256, 256), 256)
        piece = W[0, j].reshape(256, HALF)
        back[:, cols] = dot_nt(dquery[...], piece)

    def abs_of(gap):
        return jnp.sqrt(gap * gap + soft)

    spread = jnp.full((ROWS, V), MEMBERS * SOFTNESS, F32)
    miss = jnp.zeros((ROWS, V), F32)
    for m in range(MEMBERS):
        miss += abs_of(field[m] - target[...])
        for k in range(m):
            spread += 2.0 * abs_of(field[m] - field[k])
    crps = miss / MEMBERS - spread / (2.0 * MEMBERS * (MEMBERS - 1))
    share = V // MEMBERS
    crps_out[...] = pltpu.roll(crps, (V - me * share) % V, 1).T[:share, :]

    to_prev.wait_recv()
    to_next.wait_recv()
    for grad, k in ((dkey, 0), (dvalue, 1)):
        grad[pl.ds(PAIR, HALO), :] += halo_in[0, k].astype(F32)
        grad[pl.ds(HALO, HALO), :] += halo_in[1, k].astype(F32)

    @pl.loop(0, D // 256)
    def _(j):
        cols = pl.ds(pl.multiple_of(j * 256, 256), 256)
        back[:, cols] += dot_nt(dkey[inner, :].astype(BF16), W[1, j].reshape(256, HALF)) + dot_nt(
            dvalue[inner, :].astype(BF16), W[2, j].reshape(256, HALF)
        )

    back_copy = net.send(back.at[other_rows], back_in, here.at(dc=1))

    back_copy.wait_recv()

    @pl.loop(0, ROWS // 32)
    def _(i):
        rows = pl.ds(pl.multiple_of(i * 32, 32), 32)
        here_rows = pl.ds(pl.multiple_of(HALO + core * ROWS + i * 32, 32), 32)
        wide = near[here_rows, :].astype(F32)
        factor = inverse[here_rows, 0:1]
        pair_rows = pl.ds(pl.multiple_of(core * ROWS + i * 32, 32), 32)
        scaled = (back[pair_rows, :] + back_in[rows, :]) * gain[...]
        fall = dot_nt(pull[core, rows, :], w_read[...])
        middle = jnp.mean(scaled * wide, axis=-1, keepdims=True)
        grad_out[rows, :] = fall + factor * scaled - wide * (factor * factor * factor * middle)

    net.drain()


def local(latent, gain, w_query, w_key, w_value, w_read, target, neighbours, slot_mask):
    vmem, hbm = pl.BlockSpec(memory_space=pltpu.VMEM), pl.BlockSpec(memory_space=pltpu.HBM)
    crps, grad = pl.pallas_call(
        body,
        out_shape=(jax.ShapeDtypeStruct((V // MEMBERS, ROWS), F32), jax.ShapeDtypeStruct((ROWS, D), F32)),
        in_specs=[hbm] * 9,
        out_specs=(vmem, vmem),
        scratch_shapes=[
            pltpu.VMEM((1, D), F32),
            pltpu.VMEM((D, V), BF16),
            pltpu.VMEM((ROWS, V), F32),
            pltpu.VMEM((2, SLOTS, ROWS), jnp.int32),
            pltpu.VMEM((3, Y, Z_LO, 32, HALF), BF16),
            pltpu.VMEM((NEAR, D), BF16),
            pltpu.VMEM((NEAR, D), BF16),
            pltpu.VMEM((NEAR, 128), F32),
            pltpu.VMEM((2, ROWS, WINDOW), BF16),
            pltpu.VMEM((PAIR, HALF), BF16),
            pltpu.VMEM((NEAR, HALF), BF16),
            pltpu.VMEM((NEAR, HALF), BF16),
            pltpu.VMEM((2, 2, GROUPS, 2 * HALO, WINDOW), F32),
            pltpu.VMEM((PAIR, HALF), F32),
            pltpu.VMEM((PAIR, V), F32),
            pltpu.VMEM((2, HALO, V), F32),
            pltpu.VMEM((MEMBERS, ROWS, V), F32),
            pltpu.VMEM((2, ROWS, V), BF16),
            pltpu.VMEM((PAIR, HALF), BF16),
            pltpu.VMEM((PAIR, HALF), BF16),
            pltpu.VMEM((NEAR, HALF), F32),
            pltpu.VMEM((NEAR, HALF), F32),
            pltpu.VMEM((2, 2, HALO, HALF), BF16),
            pltpu.VMEM((2, 2, HALO, HALF), BF16),
            pltpu.VMEM((PAIR, D), F32),
            pltpu.VMEM((ROWS, D), F32),
            pltpu.SemaphoreType.DMA((COPIES,)),
            pltpu.SemaphoreType.DMA((COPIES,)),
            pltpu.SemaphoreType.DMA((4,)),
            pltpu.SemaphoreType.DMA((5,)),
            pltpu.SemaphoreType.REGULAR((len(TELL),)),
        ],
        compiler_params=pltpu.CompilerParams(
            collective_id=0, has_side_effects=True, vmem_limit_bytes=63 * 1024 * 1024
        ),
    )(latent[0], gain[None], w_query, w_key, w_value, w_read, target, neighbours.T, slot_mask.T)
    return crps.T, grad[None]


def solution(mesh):
    placed = (
        P("ens", "node", None),
        P(),
        P("node", None),
        P("node", None),
        P("node", None),
        P(),
        P("node", None),
        P("node", None),
        P("node", None),
    )
    return jax.shard_map(
        local,
        mesh=mesh,
        in_specs=placed,
        out_specs=(P("node", "ens"), P("ens", "node", None)),
        check_vma=False,
    )
```

```python
import jax
import jax.numpy as jnp
from jax import lax
from jax.experimental import pallas as pl
from jax.experimental.pallas import tpu as pltpu
from jax.sharding import PartitionSpec as P

HEAD_DIM = 64
SLOTS = 8
HALO = 64
EPSILON = 1e-06
SOFTNESS = 0.1

D = 1024
V = 128
ROWS = 128
PAIR = 2 * ROWS
NEAR = PAIR + 2 * HALO
HALF = D // 2
WINDOW = ROWS + 2 * HALO
GROUPS = HALF // 128
MEMBERS = 8
X, Y, Z, Z_LO = 4, 4, 16, 8
CHIPS = Y * Z_LO
MESH = pl.DeviceIdType.MESH
COPIES = 160
NEXT_TO = [dict(dc=1), dict(dy=1), dict(dy=-1), dict(dy=2), dict(dz=1), dict(dz=-1), dict(dx=1), dict(dx=-1), dict(dx=2)]
TELL = [[dict(dz=1), dict(dz=-1)], [dict(dz=2), dict(dz=-2)], [dict(dz=4), dict(dz=-4)], [dict(dy=1), dict(dy=-1)]]

F32 = jnp.float32
BF16 = jnp.bfloat16
NT = (((1,), (1,)), ((), ()))
TN = (((0,), (0,)), ((), ()))


def dot(a, b):
    return jnp.dot(a, b, preferred_element_type=F32)


def dot_nt(a, b):
    return lax.dot_general(a, b, NT, preferred_element_type=F32)


def dot_tn(a, b):
    return lax.dot_general(a, b, TN, preferred_element_type=F32)


class Place:
    def __init__(self):
        self.member = lax.axis_index("ens")
        self.node = lax.axis_index("node")
        self.x = self.member % X
        self.y = self.node // (2 * Z_LO)
        self.z = (self.member // X) * Z_LO + (self.node // 2) % Z_LO
        self.core = self.node % 2

    def at(self, dx=0, dy=0, dz=0, dc=0):
        x, y, z = (self.x + dx + X) % X, (self.y + dy + Y) % Y, (self.z + dz + Z) % Z
        core = (self.core + dc) % 2
        return {"ens": (z // Z_LO) * X + x, "node": (y * Z_LO + z % Z_LO) * 2 + core}

    def chip(self, step, core):
        return {"ens": self.member, "node": ((self.node // 2 + step + CHIPS) % CHIPS) * 2 + core}


class Net:
    def __init__(self, send_sem, recv_sem):
        self.send_sem, self.recv_sem = send_sem, recv_sem
        self.count = 0
        self.sent = []

    def send(self, src, dst, to):
        copy = pltpu.make_async_remote_copy(
            src_ref=src,
            dst_ref=dst,
            send_sem=self.send_sem.at[self.count],
            recv_sem=self.recv_sem.at[self.count],
            device_id=to,
            device_id_type=MESH,
        )
        self.count += 1
        copy.start()
        self.sent.append(copy)
        return copy

    def drain(self):
        for copy in self.sent:
            copy.wait_send()


def gather_weights(here, net, w_refs, W, local_sem, between):
    y, z, c = here.y, here.z % Z_LO, here.core
    mine, other = pl.multiple_of(c * HALF, HALF), pl.multiple_of((1 - c) * HALF, HALF)
    own_rows = pl.ds(pl.multiple_of(c * 16, 16), 16)
    local, swap = [], []
    for i, w in enumerate(w_refs):
        spot = W.at[i, y, z, own_rows]
        swap.append(net.send(w.at[:, pl.ds(other, HALF)], spot, here.at(dc=1)))
        local.append(pltpu.make_async_copy(w.at[:, pl.ds(mine, HALF)], spot, local_sem.at[i]))
        local[-1].start()
    for copy in local:
        copy.wait()
    for copy in swap:
        copy.wait_recv()

    first, second = pl.ds(0, 16), pl.ds(16, 16)
    kept = pl.ds(here.x % 2, 2)
    given = (here.x % 2) * 2
    across = []

    def pass_on(rows, ys, zs):
        piece = W.at[given, ys, zs, rows]
        across.append(net.send(piece, piece, here.at(dx=1 if rows is first else -1)))

    def forward(ys, zs, rows, **step):
        piece = W.at[kept, ys, zs, rows]
        return net.send(piece, piece, here.at(**step))

    every = slice(None)
    below, above, far = (y + 3) % Y, (y + 1) % Y, (y + 2) % Y
    def spread(zs):
        return (zs, [forward(y, zs, second, dy=d) for d in (1, -1, 2)])

    def settle(zs, copies):
        for copy in copies:
            copy.wait_recv()
        for ys in (below, above, far) if zs is z else (below, above, far, y):
            pass_on(second, ys, zs)

    def forward_first(piece, zs, **step):
        k, ys = piece
        part = W.at[here.x % 2 + k, ys, zs, first]
        return net.send(part, part, here.at(**step))

    second_up, second_down = forward(y, z, second, dz=1), forward(y, z, second, dz=-1)
    along_y = [forward(y, z, first, dy=d) for d in (1, -1, 2)]
    pending = [spread(z)]
    between[0]()
    for copy in along_y:
        copy.wait_recv()
    pieces = [(k, pl.ds(2 * j, 2)) for j in range(2) for k in range(2)]
    up = [forward_first(piece, z, dz=1) for piece in pieces]
    down = [forward_first(piece, z, dz=-1) for piece in pieces]
    for ys in (below, above, far):
        pass_on(first, ys, z)

    last = Z_LO // 2
    for step in range(1, last + 1):
        before, after = (z + Z_LO - step) % Z_LO, (z + step) % Z_LO
        arrived = []
        if step < last:
            second_up.wait_recv()
            if step < last - 1:
                second_up = forward(y, before, second, dz=1)
        second_down.wait_recv()
        if step < last:
            second_down = forward(y, after, second, dz=-1)
            arrived.append(spread(before))
        arrived.append(spread(after))
        if step < last:
            next_up, next_down = [], []
            for i, piece in enumerate(pieces):
                up[i].wait_recv()
                if step < last - 1 or i < 2:
                    next_up.append(forward_first(piece, before, dz=1))
                down[i].wait_recv()
                if step < last - 1 or i >= 2:
                    next_down.append(forward_first(piece, after, dz=-1))
            up, down = next_up, next_down
            pass_on(first, every, before)
            pass_on(first, every, after)
        else:
            for copy in up + down:
                copy.wait_recv()
            pass_on(first, every, after)
        for item in pending:
            settle(*item)
        pending = arrived
        between[step]()
    for item in pending:
        settle(*item)
    between[last + 1]()
    for copy in across:
        copy.wait_recv()


def body(
    latent, gain_in, w_query, w_key, w_value, w_read_in, target_in, neighbours, slot_mask,
    crps_out, grad_out,
    gain, w_read, target, slots,
    W, near, normed, inverse, counts, queries, keys, values, probs, mixed,
    part, part_in, field, pull, down, dquery, dkey, dvalue, halo_out, halo_in, back, back_in,
    send_sem, recv_sem, local_sem, input_sem, ready,
):
    here = Place()
    net = Net(send_sem, recv_sem)
    core = here.core
    inputs = [(gain_in, gain), (w_read_in, w_read), (target_in, target), (neighbours, slots.at[0]), (slot_mask, slots.at[1])]
    inputs = [pltpu.make_async_copy(src, dst, input_sem.at[i]) for i, (src, dst) in enumerate(inputs)]
    peers = [here.at(**step) for step in NEXT_TO]
    barrier = pltpu.get_barrier_semaphore()
    for peer in peers:
        pl.semaphore_signal(barrier, inc=1, device_id=peer, device_id_type=MESH)
    for copy in inputs:
        copy.start()
    pl.semaphore_wait(barrier, len(peers))

    own = pl.ds(pl.multiple_of(HALO + core * ROWS, 64), ROWS)
    edge = pl.ds(pl.multiple_of(core * HALO, 64), HALO)
    edge_there = pl.ds(pl.multiple_of((1 - core) * (HALO + PAIR), 64), HALO)
    edge_here = pl.ds(pl.multiple_of(core * (HALO + PAIR), 64), HALO)
    own_copy = pltpu.make_async_copy(latent, near.at[own], local_sem.at[3])
    copies = {}

    def tell(step):
        for to in TELL[step]:
            pl.semaphore_signal(ready.at[step], inc=1, device_id=here.at(**to), device_id_type=MESH)

    def hear(step):
        pl.semaphore_wait(ready.at[step], len(TELL[step]))

    def normalize(start, count):
        @pl.loop(0, count // 64)
        def _(i):
            rows = pl.ds(pl.multiple_of(start + i * 64, 64), 64)
            wide = near[rows, :].astype(F32)
            scale = lax.rsqrt(jnp.mean(wide * wide, axis=-1, keepdims=True) + EPSILON)
            inverse[rows, :] = jnp.broadcast_to(scale, (64, 128))
            normed[rows, :] = (wide * scale * gain[...]).astype(BF16)

    def count_slots():
        for copy in inputs:
            copy.wait()
        first = here.node * ROWS - HALO
        total = 2 * CHIPS * ROWS
        spot = slots[0] - first
        spot = jnp.where(spot < 0, spot + total, spot)
        spot = jnp.where(spot >= total, spot - total, spot)
        spot = jnp.where(slots[1] > 0, spot, -1).astype(F32).T
        window = lax.broadcasted_iota(jnp.int32, (ROWS, WINDOW), 1).astype(F32)
        number = jnp.zeros((ROWS, WINDOW), F32)
        for j in range(SLOTS):
            number += jnp.where(spot[:, j : j + 1] == window, 1.0, 0.0)
        counts[core] = number.astype(BF16)
        copies["count"] = net.send(counts.at[core], counts.at[core], here.at(dc=1))

    def between_0():
        own_copy.start()
        copies["pair"] = net.send(latent, near.at[own], here.at(dc=1))
        tell(0)
        count_slots()
        hear(0)
        tell(1)
        hear(1)
        tell(2)

    def between_1():
        hear(2)
        tell(3)

    def between_2():
        hear(3)
        copies["edge"] = net.send(latent.at[edge], near.at[edge_there], here.chip(2 * core - 1, 1 - core))

    def between_4():
        own_copy.wait()
        normalize(HALO + core * ROWS, ROWS)

    def between_5():
        copies["edge"].wait_recv()
        copies["hand_on"] = net.send(near.at[edge_here], near.at[edge_here], here.at(dc=1))
        copies["pair"].wait_recv()
        normalize(HALO + (1 - core) * ROWS, ROWS)
        normalize(core * (HALO + PAIR), HALO)
        copies["hand_on"].wait_recv()
        normalize((1 - core) * (HALO + PAIR), HALO)
        copies["count"].wait_recv()

    between = [between_0, between_1, between_2, lambda: None, between_4, between_5]
    gather_weights(here, net, (w_query, w_key, w_value), W, local_sem, between)

    inner = pl.ds(HALO, PAIR)

    @pl.loop(0, HALF // 256)
    def _(j):
        cols = pl.ds(pl.multiple_of(j * 256, 256), 256)
        queries[:, cols] = dot(normed[inner, :], W[0, :, :, :, cols].reshape(D, 256)).astype(BF16)
        keys[:, cols] = dot(normed[...], W[1, :, :, :, cols].reshape(D, 256)).astype(BF16)
        values[:, cols] = dot(normed[...], W[2, :, :, :, cols].reshape(D, 256)).astype(BF16)

    lanes = lax.broadcasted_iota(jnp.int32, (1, 128), 1)
    low = (lanes < HEAD_DIM).astype(F32)
    low_b, high_b = low.astype(BF16), (1.0 - low).astype(BF16)
    scale = HEAD_DIM ** (-0.5)

    def two_heads(piece):
        return jnp.concatenate([piece * low_b, piece * high_b], axis=0)

    def one_piece(both):
        return jnp.where(lanes < HEAD_DIM, both[:HALO], both[HALO:])

    def start_of(half, block):
        return block * ROWS + HALO * ((half + block) % 2)

    def places(half, block, group):
        rows = pl.ds(start_of(half, block), HALO)
        around = pl.ds(block * ROWS, WINDOW)
        return rows, around, pl.ds(pl.multiple_of(group * 128, 128), 128)

    def count_of(half, block):
        one = counts[block, pl.ds(HALO * ((half + block) % 2), HALO), :].astype(F32)
        return jnp.concatenate([one, one], axis=0)

    mine = pl.ds(pl.multiple_of(core * HALF, HALF), HALF)
    me = here.member
    partner = (me + X) % MEMBERS
    fields = [{}, {}]

    def own_rows(half, offset=0, count=HALO):
        return pl.ds(pl.multiple_of(HALO * ((half + core) % 2) + offset, 32), count)

    def attend(half):
        @pl.loop(0, GROUPS)
        def _(group):
            for block in range(2):
                rows, around, cols = places(half, block, group)
                number = count_of(half, block)
                scores = dot_nt(two_heads(queries[rows, cols]), keys[around, cols])
                weight = jnp.where(number > 0, jnp.exp(scores * scale), 0.0)
                prob = weight / jnp.sum(number * weight, axis=-1, keepdims=True)
                probs[half, block, group] = prob
                share = (prob.astype(BF16).astype(F32) * number).astype(BF16)
                mixed[rows, cols] = one_piece(dot(share, values[around, cols]))

    def read_out(half):
        for block in range(2):
            rows = pl.ds(start_of(half, block), HALO)
            wide = near[pl.ds(HALO + start_of(half, block), HALO), mine].astype(F32)
            part[rows, :] = dot((wide + mixed[rows, :]).astype(BF16), w_read[mine, :])
        theirs = pl.ds(pl.multiple_of((1 - core) * ROWS + HALO * ((half + 1 - core) % 2), 64), HALO)
        ours = pl.ds(pl.multiple_of(core * ROWS + HALO * ((half + core) % 2), 64), HALO)
        net.send(part.at[theirs], part_in.at[half], here.at(dc=1)).wait_recv()
        field[me, own_rows(half), :] = part[ours, :] + part_in[half]
        pieces = [field.at[me, own_rows(half, 32 * k, 32)] for k in range(2)]
        fields[half]["over"] = [net.send(piece, piece, here.at(dz=8)) for piece in pieces]
        whole = field.at[me, own_rows(half)]
        fields[half]["along"] = [net.send(whole, whole, here.at(dx=d)) for d in (1, -1, 2)]

    def relay(half):
        for k, copy in enumerate(fields[half]["over"]):
            copy.wait_recv()
            piece = field.at[partner, own_rows(half, 32 * k, 32)]
            fields[half]["along"] += [net.send(piece, piece, here.at(dx=d)) for d in (1, -1, 2)]

    soft = SOFTNESS * SOFTNESS

    def sign_of(gap):
        return gap * lax.rsqrt(gap * gap + soft)

    def pull_back(half):
        for copy in fields[half]["along"]:
            copy.wait_recv()
        rows = own_rows(half)
        here_field = field[me, rows, :]
        returned = sign_of(here_field - field[0, rows, :])
        for m in range(1, MEMBERS):
            returned += sign_of(here_field - field[m, rows, :])
        pulled = sign_of(here_field - target[rows, :]) - returned / (MEMBERS - 1)
        pull[core, rows, :] = pulled.astype(BF16)
        piece = pull.at[core, rows]
        net.send(piece, piece, here.at(dc=1)).wait_recv()
        for block in range(2):
            there = pull[block, pl.ds(HALO * ((half + block) % 2), HALO), :]
            down[pl.ds(start_of(half, block), HALO), :] = dot_nt(there, w_read[mine, :]).astype(BF16)

    def backward(half, after=None):
        def one_group(group):
            for block in range(2):
                rows, around, cols = places(half, block, group)
                number = count_of(half, block)
                prob = probs[half, block, group]
                given = two_heads(down[rows, cols])
                asked = two_heads(queries[rows, cols])
                share = (prob.astype(BF16).astype(F32) * number).astype(BF16)
                dprob = dot_nt(given, values[around, cols])
                level = jnp.sum(number * prob * dprob, axis=-1, keepdims=True)
                dscaled = (prob * (dprob - level) * scale).astype(BF16)
                dscaled = (dscaled.astype(F32) * number).astype(BF16)
                dquery[rows, cols] = one_piece(dot(dscaled, keys[around, cols])).astype(BF16)
                dkey[around, cols] += dot_tn(dscaled, asked)
                dvalue[around, cols] += dot_tn(share, given)

        if after is None:
            pl.loop(0, GROUPS)(one_group)
        else:
            for group in range(GROUPS):
                one_group(group)
                after(group)

    halos = []

    def send_halos(group):
        cols = pl.ds(group * 128, 128)
        for side, rows, step in ((0, pl.ds(0, HALO), -1), (1, pl.ds(HALO + PAIR, HALO), 1)):
            halo_out[side, 0, :, cols] = dkey[rows, cols].astype(BF16)
            halo_out[side, 1, :, cols] = dvalue[rows, cols].astype(BF16)
            piece = (side, slice(None), slice(None), cols)
            halos.append(net.send(halo_out.at[piece], halo_in.at[piece], here.chip(step, core)))

    for half in range(2):
        attend(half)
        read_out(half)
    dkey[...] = jnp.zeros_like(dkey)
    dvalue[...] = jnp.zeros_like(dvalue)
    relay(0)
    relay(1)
    pull_back(0)
    backward(0, send_halos)
    pull_back(1)
    backward(1)

    mine_rows = pl.ds(pl.multiple_of(core * ROWS, ROWS), ROWS)
    other_rows = pl.ds(pl.multiple_of((1 - core) * ROWS, ROWS), ROWS)

    @pl.loop(0, D // 256)
    def _(j):
        cols = pl.ds(pl.multiple_of(j * 256, 256), 256)
        piece = W[0, j].reshape(256, HALF)
        back[:, cols] = dot_nt(dquery[...], piece)

    def abs_of(gap):
        return jnp.sqrt(gap * gap + soft)

    spread = jnp.full((ROWS, V), MEMBERS * SOFTNESS, F32)
    miss = jnp.zeros((ROWS, V), F32)
    for m in range(MEMBERS):
        miss += abs_of(field[m] - target[...])
        for k in range(m):
            spread += 2.0 * abs_of(field[m] - field[k])
    crps = miss / MEMBERS - spread / (2.0 * MEMBERS * (MEMBERS - 1))
    share = V // MEMBERS
    crps_out[...] = pltpu.roll(crps, (V - me * share) % V, 1).T[:share, :]

    for copy in halos:
        copy.wait_recv()
    for grad, k in ((dkey, 0), (dvalue, 1)):
        grad[pl.ds(PAIR, HALO), :] += halo_in[0, k].astype(F32)
        grad[pl.ds(HALO, HALO), :] += halo_in[1, k].astype(F32)

    back_copies = []
    for j in range(D // 256):
        cols = pl.ds(j * 256, 256)
        back[:, cols] += dot_nt(dkey[inner, :].astype(BF16), W[1, j].reshape(256, HALF)) + dot_nt(
            dvalue[inner, :].astype(BF16), W[2, j].reshape(256, HALF)
        )
        back_copies.append(net.send(back.at[other_rows, cols], back_in.at[:, cols], here.at(dc=1)))
    for copy in back_copies:
        copy.wait_recv()

    @pl.loop(0, ROWS // 32)
    def _(i):
        rows = pl.ds(pl.multiple_of(i * 32, 32), 32)
        here_rows = pl.ds(pl.multiple_of(HALO + core * ROWS + i * 32, 32), 32)
        wide = near[here_rows, :].astype(F32)
        factor = inverse[here_rows, 0:1]
        pair_rows = pl.ds(pl.multiple_of(core * ROWS + i * 32, 32), 32)
        scaled = (back[pair_rows, :] + back_in[rows, :]) * gain[...]
        fall = dot_nt(pull[core, rows, :], w_read[...])
        middle = jnp.mean(scaled * wide, axis=-1, keepdims=True)
        grad_out[rows, :] = fall + factor * scaled - wide * (factor * factor * factor * middle)

    net.drain()


def local(latent, gain, w_query, w_key, w_value, w_read, target, neighbours, slot_mask):
    vmem, hbm = pl.BlockSpec(memory_space=pltpu.VMEM), pl.BlockSpec(memory_space=pltpu.HBM)
    crps, grad = pl.pallas_call(
        body,
        out_shape=(jax.ShapeDtypeStruct((V // MEMBERS, ROWS), F32), jax.ShapeDtypeStruct((ROWS, D), F32)),
        in_specs=[hbm] * 9,
        out_specs=(vmem, vmem),
        scratch_shapes=[
            pltpu.VMEM((1, D), F32),
            pltpu.VMEM((D, V), BF16),
            pltpu.VMEM((ROWS, V), F32),
            pltpu.VMEM((2, SLOTS, ROWS), jnp.int32),
            pltpu.VMEM((3, Y, Z_LO, 32, HALF), BF16),
            pltpu.VMEM((NEAR, D), BF16),
            pltpu.VMEM((NEAR, D), BF16),
            pltpu.VMEM((NEAR, 128), F32),
            pltpu.VMEM((2, ROWS, WINDOW), BF16),
            pltpu.VMEM((PAIR, HALF), BF16),
            pltpu.VMEM((NEAR, HALF), BF16),
            pltpu.VMEM((NEAR, HALF), BF16),
            pltpu.VMEM((2, 2, GROUPS, 2 * HALO, WINDOW), F32),
            pltpu.VMEM((PAIR, HALF), F32),
            pltpu.VMEM((PAIR, V), F32),
            pltpu.VMEM((2, HALO, V), F32),
            pltpu.VMEM((MEMBERS, ROWS, V), F32),
            pltpu.VMEM((2, ROWS, V), BF16),
            pltpu.VMEM((PAIR, HALF), BF16),
            pltpu.VMEM((PAIR, HALF), BF16),
            pltpu.VMEM((NEAR, HALF), F32),
            pltpu.VMEM((NEAR, HALF), F32),
            pltpu.VMEM((2, 2, HALO, HALF), BF16),
            pltpu.VMEM((2, 2, HALO, HALF), BF16),
            pltpu.VMEM((PAIR, D), F32),
            pltpu.VMEM((ROWS, D), F32),
            pltpu.SemaphoreType.DMA((COPIES,)),
            pltpu.SemaphoreType.DMA((COPIES,)),
            pltpu.SemaphoreType.DMA((4,)),
            pltpu.SemaphoreType.DMA((5,)),
            pltpu.SemaphoreType.REGULAR((len(TELL),)),
        ],
        compiler_params=pltpu.CompilerParams(
            collective_id=0, has_side_effects=True, vmem_limit_bytes=63 * 1024 * 1024
        ),
    )(latent[0], gain[None], w_query, w_key, w_value, w_read, target, neighbours.T, slot_mask.T)
    return crps.T, grad[None]


def solution(mesh):
    placed = (
        P("ens", "node", None),
        P(),
        P("node", None),
        P("node", None),
        P("node", None),
        P(),
        P("node", None),
        P("node", None),
        P("node", None),
    )
    return jax.shard_map(
        local,
        mesh=mesh,
        in_specs=placed,
        out_specs=(P("node", "ens"), P("ens", "node", None)),
        check_vma=False,
    )
```

```python
import jax
import jax.numpy as jnp
from jax import lax
from jax.experimental import pallas as pl
from jax.experimental.pallas import tpu as pltpu
from jax.sharding import PartitionSpec as P

HEAD_DIM = 64
SLOTS = 8
HALO = 64
EPSILON = 1e-06
SOFTNESS = 0.1

D = 1024
V = 128
ROWS = 128
PAIR = 2 * ROWS
NEAR = PAIR + 2 * HALO
HALF = D // 2
WINDOW = ROWS + 2 * HALO
GROUPS = HALF // 128
MEMBERS = 8
X, Y, Z, Z_LO = 4, 4, 16, 8
CHIPS = Y * Z_LO
MESH = pl.DeviceIdType.MESH
COPIES = 160
NEXT_TO = [dict(dc=1), dict(dy=1), dict(dy=-1), dict(dy=2), dict(dz=1), dict(dz=-1), dict(dx=1), dict(dx=-1), dict(dx=2)]
TELL = [[dict(dz=1), dict(dz=-1)], [dict(dz=2), dict(dz=-2)], [dict(dz=4), dict(dz=-4)], [dict(dy=1), dict(dy=-1)]]

F32 = jnp.float32
BF16 = jnp.bfloat16
NT = (((1,), (1,)), ((), ()))
TN = (((0,), (0,)), ((), ()))


def dot(a, b):
    return jnp.dot(a, b, preferred_element_type=F32)


def dot_nt(a, b):
    return lax.dot_general(a, b, NT, preferred_element_type=F32)


def dot_tn(a, b):
    return lax.dot_general(a, b, TN, preferred_element_type=F32)


class Place:
    def __init__(self):
        self.member = lax.axis_index("ens")
        self.node = lax.axis_index("node")
        self.x = self.member % X
        self.y = self.node // (2 * Z_LO)
        self.z = (self.member // X) * Z_LO + (self.node // 2) % Z_LO
        self.core = self.node % 2

    def at(self, dx=0, dy=0, dz=0, dc=0):
        x, y, z = (self.x + dx + X) % X, (self.y + dy + Y) % Y, (self.z + dz + Z) % Z
        core = (self.core + dc) % 2
        return {"ens": (z // Z_LO) * X + x, "node": (y * Z_LO + z % Z_LO) * 2 + core}

    def chip(self, step, core):
        return {"ens": self.member, "node": ((self.node // 2 + step + CHIPS) % CHIPS) * 2 + core}


class Net:
    def __init__(self, send_sem, recv_sem):
        self.send_sem, self.recv_sem = send_sem, recv_sem
        self.count = 0
        self.sent = []

    def send(self, src, dst, to):
        copy = pltpu.make_async_remote_copy(
            src_ref=src,
            dst_ref=dst,
            send_sem=self.send_sem.at[self.count],
            recv_sem=self.recv_sem.at[self.count],
            device_id=to,
            device_id_type=MESH,
        )
        self.count += 1
        copy.start()
        self.sent.append(copy)
        return copy

    def drain(self):
        for copy in self.sent:
            copy.wait_send()


def gather_weights(here, net, w_refs, W, local_sem, between):
    y, z, c = here.y, here.z % Z_LO, here.core
    mine, other = pl.multiple_of(c * HALF, HALF), pl.multiple_of((1 - c) * HALF, HALF)
    own_rows = pl.ds(pl.multiple_of(c * 16, 16), 16)
    local, swap = [], []
    for i, w in enumerate(w_refs):
        spot = W.at[i, y, z, own_rows]
        swap.append(net.send(w.at[:, pl.ds(other, HALF)], spot, here.at(dc=1)))
        local.append(pltpu.make_async_copy(w.at[:, pl.ds(mine, HALF)], spot, local_sem.at[i]))
        local[-1].start()
    for copy in local:
        copy.wait()
    for copy in swap:
        copy.wait_recv()

    first, second = pl.ds(0, 16), pl.ds(16, 16)
    kept = pl.ds(here.x % 2, 2)
    given = (here.x % 2) * 2
    across = []

    def pass_on(rows, ys, zs):
        piece = W.at[given, ys, zs, rows]
        across.append(net.send(piece, piece, here.at(dx=1 if rows is first else -1)))

    def forward(ys, zs, rows, **step):
        piece = W.at[kept, ys, zs, rows]
        return net.send(piece, piece, here.at(**step))

    every = slice(None)
    below, above, far = (y + 3) % Y, (y + 1) % Y, (y + 2) % Y
    def spread(zs):
        return (zs, [forward(y, zs, second, dy=d) for d in (1, -1, 2)])

    def settle(zs, copies):
        for copy in copies:
            copy.wait_recv()
        for ys in (below, above, far) if zs is z else (below, above, far, y):
            pass_on(second, ys, zs)

    def forward_first(piece, zs, **step):
        k, ys = piece
        part = W.at[here.x % 2 + k, ys, zs, first]
        return net.send(part, part, here.at(**step))

    second_up, second_down = forward(y, z, second, dz=1), forward(y, z, second, dz=-1)
    along_y = [forward(y, z, first, dy=d) for d in (1, -1, 2)]
    pending = [spread(z)]
    between[0]()
    for copy in along_y:
        copy.wait_recv()
    pieces = [(k, pl.ds(2 * j, 2)) for j in range(2) for k in range(2)]
    up = [forward_first(piece, z, dz=1) for piece in pieces]
    down = [forward_first(piece, z, dz=-1) for piece in pieces]
    for ys in (below, above, far):
        pass_on(first, ys, z)

    last = Z_LO // 2
    for step in range(1, last + 1):
        before, after = (z + Z_LO - step) % Z_LO, (z + step) % Z_LO
        arrived = []
        if step < last:
            second_up.wait_recv()
            if step < last - 1:
                second_up = forward(y, before, second, dz=1)
        second_down.wait_recv()
        if step < last:
            second_down = forward(y, after, second, dz=-1)
            arrived.append(spread(before))
        arrived.append(spread(after))
        if step < last:
            next_up, next_down = [], []
            for i, piece in enumerate(pieces):
                up[i].wait_recv()
                if step < last - 1 or i < 2:
                    next_up.append(forward_first(piece, before, dz=1))
                down[i].wait_recv()
                if step < last - 1 or i >= 2:
                    next_down.append(forward_first(piece, after, dz=-1))
            up, down = next_up, next_down
            pass_on(first, every, before)
            pass_on(first, every, after)
        else:
            for copy in up + down:
                copy.wait_recv()
            pass_on(first, every, after)
        for item in pending:
            settle(*item)
        pending = arrived
        between[step]()
    for item in pending:
        settle(*item)
    between[last + 1]()
    for copy in across:
        copy.wait_recv()


def body(
    latent, gain_in, w_query, w_key, w_value, w_read_in, target_in, neighbours, slot_mask,
    crps_out, grad_out,
    gain, w_read, target, slots,
    W, near, normed, inverse, counts, queries, keys, values, probs, mixed,
    part, part_in, field, pull, down, dquery, dkey, dvalue, halo_out, halo_in, back, back_in,
    send_sem, recv_sem, local_sem, input_sem, ready,
):
    here = Place()
    net = Net(send_sem, recv_sem)
    core = here.core
    inputs = [(gain_in, gain), (w_read_in, w_read), (target_in, target), (neighbours, slots.at[0]), (slot_mask, slots.at[1])]
    inputs = [pltpu.make_async_copy(src, dst, input_sem.at[i]) for i, (src, dst) in enumerate(inputs)]
    peers = [here.at(**step) for step in NEXT_TO]
    barrier = pltpu.get_barrier_semaphore()
    for peer in peers:
        pl.semaphore_signal(barrier, inc=1, device_id=peer, device_id_type=MESH)
    for copy in inputs:
        copy.start()
    pl.semaphore_wait(barrier, len(peers))

    own = pl.ds(pl.multiple_of(HALO + core * ROWS, 64), ROWS)
    edge = pl.ds(pl.multiple_of(core * HALO, 64), HALO)
    edge_there = pl.ds(pl.multiple_of((1 - core) * (HALO + PAIR), 64), HALO)
    edge_here = pl.ds(pl.multiple_of(core * (HALO + PAIR), 64), HALO)
    own_copy = pltpu.make_async_copy(latent, near.at[own], local_sem.at[3])
    copies = {}

    def tell(step):
        for to in TELL[step]:
            pl.semaphore_signal(ready.at[step], inc=1, device_id=here.at(**to), device_id_type=MESH)

    def hear(step):
        pl.semaphore_wait(ready.at[step], len(TELL[step]))

    def normalize(start, count):
        @pl.loop(0, count // 64)
        def _(i):
            rows = pl.ds(pl.multiple_of(start + i * 64, 64), 64)
            wide = near[rows, :].astype(F32)
            scale = lax.rsqrt(jnp.mean(wide * wide, axis=-1, keepdims=True) + EPSILON)
            inverse[rows, :] = jnp.broadcast_to(scale, (64, 128))
            normed[rows, :] = (wide * scale * gain[...]).astype(BF16)

    def count_slots():
        for copy in inputs:
            copy.wait()
        first = here.node * ROWS - HALO
        total = 2 * CHIPS * ROWS
        spot = slots[0] - first
        spot = jnp.where(spot < 0, spot + total, spot)
        spot = jnp.where(spot >= total, spot - total, spot)
        spot = jnp.where(slots[1] > 0, spot, -1).astype(F32).T
        window = lax.broadcasted_iota(jnp.int32, (ROWS, WINDOW), 1).astype(F32)
        number = jnp.zeros((ROWS, WINDOW), F32)
        for j in range(SLOTS):
            number += jnp.where(spot[:, j : j + 1] == window, 1.0, 0.0)
        counts[core] = number.astype(BF16)
        copies["count"] = net.send(counts.at[core], counts.at[core], here.at(dc=1))

    def between_0():
        own_copy.start()
        copies["pair"] = net.send(latent, near.at[own], here.at(dc=1))
        tell(0)
        count_slots()
        hear(0)
        tell(1)
        hear(1)
        tell(2)

    def between_1():
        hear(2)
        tell(3)

    def between_2():
        hear(3)
        copies["edge"] = net.send(latent.at[edge], near.at[edge_there], here.chip(2 * core - 1, 1 - core))

    def between_4():
        own_copy.wait()
        normalize(HALO + core * ROWS, ROWS)

    def between_5():
        copies["edge"].wait_recv()
        copies["hand_on"] = net.send(near.at[edge_here], near.at[edge_here], here.at(dc=1))
        copies["pair"].wait_recv()
        normalize(HALO + (1 - core) * ROWS, ROWS)
        normalize(core * (HALO + PAIR), HALO)
        copies["hand_on"].wait_recv()
        normalize((1 - core) * (HALO + PAIR), HALO)
        copies["count"].wait_recv()

    between = [between_0, between_1, between_2, lambda: None, between_4, between_5]
    gather_weights(here, net, (w_query, w_key, w_value), W, local_sem, between)

    inner = pl.ds(HALO, PAIR)

    @pl.loop(0, HALF // 256)
    def _(j):
        cols = pl.ds(pl.multiple_of(j * 256, 256), 256)
        queries[:, cols] = dot(normed[inner, :], W[0, :, :, :, cols].reshape(D, 256)).astype(BF16)
        keys[:, cols] = dot(normed[...], W[1, :, :, :, cols].reshape(D, 256)).astype(BF16)
        values[:, cols] = dot(normed[...], W[2, :, :, :, cols].reshape(D, 256)).astype(BF16)

    lanes = lax.broadcasted_iota(jnp.int32, (1, 128), 1)
    low = (lanes < HEAD_DIM).astype(F32)
    low_b, high_b = low.astype(BF16), (1.0 - low).astype(BF16)
    scale = HEAD_DIM ** (-0.5)

    def two_heads(piece):
        return jnp.concatenate([piece * low_b, piece * high_b], axis=0)

    def one_piece(both):
        return jnp.where(lanes < HEAD_DIM, both[:HALO], both[HALO:])

    def start_of(half, block):
        return block * ROWS + HALO * ((half + block) % 2)

    def places(half, block, group):
        rows = pl.ds(start_of(half, block), HALO)
        around = pl.ds(block * ROWS, WINDOW)
        return rows, around, pl.ds(pl.multiple_of(group * 128, 128), 128)

    def count_of(half, block):
        one = counts[block, pl.ds(HALO * ((half + block) % 2), HALO), :].astype(F32)
        return jnp.concatenate([one, one], axis=0)

    mine = pl.ds(pl.multiple_of(core * HALF, HALF), HALF)
    me = here.member
    partner = (me + X) % MEMBERS
    fields = [{}, {}]

    def own_rows(half, offset=0, count=HALO):
        return pl.ds(pl.multiple_of(HALO * ((half + core) % 2) + offset, 32), count)

    def attend(half):
        for group in range(GROUPS):
            for block in range(2):
                rows, around, cols = places(half, block, group)
                number = count_of(half, block)
                scores = dot_nt(two_heads(queries[rows, cols]), keys[around, cols])
                weight = jnp.where(number > 0, jnp.exp(scores * scale), 0.0)
                prob = weight / jnp.sum(number * weight, axis=-1, keepdims=True)
                probs[half, block, group] = prob
                share = (prob.astype(BF16).astype(F32) * number).astype(BF16)
                mixed[rows, cols] = one_piece(dot(share, values[around, cols]))

    def read_out(half):
        for block in range(2):
            rows = pl.ds(start_of(half, block), HALO)
            wide = near[pl.ds(HALO + start_of(half, block), HALO), mine].astype(F32)
            part[rows, :] = dot((wide + mixed[rows, :]).astype(BF16), w_read[mine, :])
        theirs = pl.ds(pl.multiple_of((1 - core) * ROWS + HALO * ((half + 1 - core) % 2), 64), HALO)
        ours = pl.ds(pl.multiple_of(core * ROWS + HALO * ((half + core) % 2), 64), HALO)
        net.send(part.at[theirs], part_in.at[half], here.at(dc=1)).wait_recv()
        field[me, own_rows(half), :] = part[ours, :] + part_in[half]
        pieces = [field.at[me, own_rows(half, 32 * k, 32)] for k in range(2)]
        fields[half]["over"] = [net.send(piece, piece, here.at(dz=8)) for piece in pieces]
        whole = field.at[me, own_rows(half)]
        fields[half]["along"] = [net.send(whole, whole, here.at(dx=d)) for d in (1, -1, 2)]

    def relay(half):
        for k, copy in enumerate(fields[half]["over"]):
            copy.wait_recv()
            piece = field.at[partner, own_rows(half, 32 * k, 32)]
            fields[half]["along"] += [net.send(piece, piece, here.at(dx=d)) for d in (1, -1, 2)]

    soft = SOFTNESS * SOFTNESS

    def sign_of(gap):
        return gap * lax.rsqrt(gap * gap + soft)

    def pull_back(half):
        for copy in fields[half]["along"]:
            copy.wait_recv()
        rows = own_rows(half)
        here_field = field[me, rows, :]
        returned = sign_of(here_field - field[0, rows, :])
        for m in range(1, MEMBERS):
            returned += sign_of(here_field - field[m, rows, :])
        pulled = sign_of(here_field - target[rows, :]) - returned / (MEMBERS - 1)
        pull[core, rows, :] = pulled.astype(BF16)
        piece = pull.at[core, rows]
        net.send(piece, piece, here.at(dc=1)).wait_recv()
        for block in range(2):
            there = pull[block, pl.ds(HALO * ((half + block) % 2), HALO), :]
            down[pl.ds(start_of(half, block), HALO), :] = dot_nt(there, w_read[mine, :]).astype(BF16)

    def backward(half, after=None):
        def one_group(group):
            for block in range(2):
                rows, around, cols = places(half, block, group)
                number = count_of(half, block)
                prob = probs[half, block, group]
                given = two_heads(down[rows, cols])
                asked = two_heads(queries[rows, cols])
                share = (prob.astype(BF16).astype(F32) * number).astype(BF16)
                dprob = dot_nt(given, values[around, cols])
                level = jnp.sum(number * prob * dprob, axis=-1, keepdims=True)
                dscaled = (prob * (dprob - level) * scale).astype(BF16)
                dscaled = (dscaled.astype(F32) * number).astype(BF16)
                dquery[rows, cols] = one_piece(dot(dscaled, keys[around, cols])).astype(BF16)
                dkey[around, cols] += dot_tn(dscaled, asked)
                dvalue[around, cols] += dot_tn(share, given)

        if after is None:
            for group in range(GROUPS):
                one_group(group)
        else:
            for group in range(GROUPS):
                one_group(group)
                after(group)

    halos = []

    def send_halos(group):
        cols = pl.ds(group * 128, 128)
        for side, rows, step in ((0, pl.ds(0, HALO), -1), (1, pl.ds(HALO + PAIR, HALO), 1)):
            halo_out[side, 0, :, cols] = dkey[rows, cols].astype(BF16)
            halo_out[side, 1, :, cols] = dvalue[rows, cols].astype(BF16)
            piece = (side, slice(None), slice(None), cols)
            halos.append(net.send(halo_out.at[piece], halo_in.at[piece], here.chip(step, core)))

    for half in range(2):
        attend(half)
        read_out(half)
    dkey[...] = jnp.zeros_like(dkey)
    dvalue[...] = jnp.zeros_like(dvalue)
    relay(0)
    relay(1)
    pull_back(0)
    backward(0, send_halos)
    pull_back(1)
    backward(1)

    mine_rows = pl.ds(pl.multiple_of(core * ROWS, ROWS), ROWS)
    other_rows = pl.ds(pl.multiple_of((1 - core) * ROWS, ROWS), ROWS)

    @pl.loop(0, D // 256)
    def _(j):
        cols = pl.ds(pl.multiple_of(j * 256, 256), 256)
        piece = W[0, j].reshape(256, HALF)
        back[:, cols] = dot_nt(dquery[...], piece)

    def abs_of(gap):
        return jnp.sqrt(gap * gap + soft)

    spread = jnp.full((ROWS, V), MEMBERS * SOFTNESS, F32)
    miss = jnp.zeros((ROWS, V), F32)
    for m in range(MEMBERS):
        miss += abs_of(field[m] - target[...])
        for k in range(m):
            spread += 2.0 * abs_of(field[m] - field[k])
    crps = miss / MEMBERS - spread / (2.0 * MEMBERS * (MEMBERS - 1))
    share = V // MEMBERS
    crps_out[...] = pltpu.roll(crps, (V - me * share) % V, 1).T[:share, :]

    for copy in halos:
        copy.wait_recv()
    for grad, k in ((dkey, 0), (dvalue, 1)):
        grad[pl.ds(PAIR, HALO), :] += halo_in[0, k].astype(F32)
        grad[pl.ds(HALO, HALO), :] += halo_in[1, k].astype(F32)

    back_copies = []
    for j in range(D // 256):
        cols = pl.ds(j * 256, 256)
        back[:, cols] += dot_nt(dkey[inner, :].astype(BF16), W[1, j].reshape(256, HALF)) + dot_nt(
            dvalue[inner, :].astype(BF16), W[2, j].reshape(256, HALF)
        )
        back_copies.append(net.send(back.at[other_rows, cols], back_in.at[:, cols], here.at(dc=1)))
    for copy in back_copies:
        copy.wait_recv()

    @pl.loop(0, ROWS // 32)
    def _(i):
        rows = pl.ds(pl.multiple_of(i * 32, 32), 32)
        here_rows = pl.ds(pl.multiple_of(HALO + core * ROWS + i * 32, 32), 32)
        wide = near[here_rows, :].astype(F32)
        factor = inverse[here_rows, 0:1]
        pair_rows = pl.ds(pl.multiple_of(core * ROWS + i * 32, 32), 32)
        scaled = (back[pair_rows, :] + back_in[rows, :]) * gain[...]
        fall = dot_nt(pull[core, rows, :], w_read[...])
        middle = jnp.mean(scaled * wide, axis=-1, keepdims=True)
        grad_out[rows, :] = fall + factor * scaled - wide * (factor * factor * factor * middle)

    net.drain()


def local(latent, gain, w_query, w_key, w_value, w_read, target, neighbours, slot_mask):
    vmem, hbm = pl.BlockSpec(memory_space=pltpu.VMEM), pl.BlockSpec(memory_space=pltpu.HBM)
    crps, grad = pl.pallas_call(
        body,
        out_shape=(jax.ShapeDtypeStruct((V // MEMBERS, ROWS), F32), jax.ShapeDtypeStruct((ROWS, D), F32)),
        in_specs=[hbm] * 9,
        out_specs=(vmem, vmem),
        scratch_shapes=[
            pltpu.VMEM((1, D), F32),
            pltpu.VMEM((D, V), BF16),
            pltpu.VMEM((ROWS, V), F32),
            pltpu.VMEM((2, SLOTS, ROWS), jnp.int32),
            pltpu.VMEM((3, Y, Z_LO, 32, HALF), BF16),
            pltpu.VMEM((NEAR, D), BF16),
            pltpu.VMEM((NEAR, D), BF16),
            pltpu.VMEM((NEAR, 128), F32),
            pltpu.VMEM((2, ROWS, WINDOW), BF16),
            pltpu.VMEM((PAIR, HALF), BF16),
            pltpu.VMEM((NEAR, HALF), BF16),
            pltpu.VMEM((NEAR, HALF), BF16),
            pltpu.VMEM((2, 2, GROUPS, 2 * HALO, WINDOW), F32),
            pltpu.VMEM((PAIR, HALF), F32),
            pltpu.VMEM((PAIR, V), F32),
            pltpu.VMEM((2, HALO, V), F32),
            pltpu.VMEM((MEMBERS, ROWS, V), F32),
            pltpu.VMEM((2, ROWS, V), BF16),
            pltpu.VMEM((PAIR, HALF), BF16),
            pltpu.VMEM((PAIR, HALF), BF16),
            pltpu.VMEM((NEAR, HALF), F32),
            pltpu.VMEM((NEAR, HALF), F32),
            pltpu.VMEM((2, 2, HALO, HALF), BF16),
            pltpu.VMEM((2, 2, HALO, HALF), BF16),
            pltpu.VMEM((PAIR, D), F32),
            pltpu.VMEM((ROWS, D), F32),
            pltpu.SemaphoreType.DMA((COPIES,)),
            pltpu.SemaphoreType.DMA((COPIES,)),
            pltpu.SemaphoreType.DMA((4,)),
            pltpu.SemaphoreType.DMA((5,)),
            pltpu.SemaphoreType.REGULAR((len(TELL),)),
        ],
        compiler_params=pltpu.CompilerParams(
            collective_id=0, has_side_effects=True, vmem_limit_bytes=63 * 1024 * 1024
        ),
    )(latent[0], gain[None], w_query, w_key, w_value, w_read, target, neighbours.T, slot_mask.T)
    return crps.T, grad[None]


def solution(mesh):
    placed = (
        P("ens", "node", None),
        P(),
        P("node", None),
        P("node", None),
        P("node", None),
        P(),
        P("node", None),
        P("node", None),
        P("node", None),
    )
    return jax.shard_map(
        local,
        mesh=mesh,
        in_specs=placed,
        out_specs=(P("node", "ens"), P("ens", "node", None)),
        check_vma=False,
    )
```
